32 devices in a mesh: dp: 2 (over y), seq: 4 (over z), mp: 4 (over x, core).
Axes of the slice: x: 2, y: 2, z: 4, core: 2. Of those that a mesh axis runs over, the one named last changes fastest.
Arguments:
- hidden_in: bfloat16 [4, 4096, 768], P('dp', 'seq'), may hold values from -6 to 6
- segments: int32 [4, 4096], P('dp', 'seq'), may hold values from 0 to 3, as said below
- cotangent: bfloat16 [4, 4096, 768], P('dp', 'seq'), may hold values from -6 to 6
- qkv_weight: bfloat16 [768, 3, 768], P(('dp', 'seq'), None, 'mp'), may hold values from -0.21875 to 0.21875
- qv_bias: float32 [2, 768], P(None, 'mp'), may hold values from -3 to 3
- proj_weight: bfloat16 [768, 768], P(('dp', 'seq'), 'mp'), may hold values from -0.875 to 0.875
- proj_bias: float32 [768], replicated, may hold values from -2 to 2
- first_gain: float32 [768], replicated, may hold values from 0.5 to 1.5
- first_shift: float32 [768], replicated, may hold values from -2 to 2
- up_weight: bfloat16 [768, 3072], P(('dp', 'seq'), 'mp'), may hold values from -0.21875 to 0.21875
- up_bias: float32 [3072], P('mp'), may hold values from -3 to 3
- down_weight: bfloat16 [768, 3072], P(('dp', 'seq'), 'mp'), may hold values from -0.109375 to 0.109375
- down_bias: float32 [768], replicated, may hold values from -2 to 2
- second_gain: float32 [768], replicated, may hold values from 0.5 to 1.5
- second_shift: float32 [768], replicated, may hold values from -2 to 2
Outputs:
- layer_out: bfloat16 [4, 4096, 768], P('dp', 'seq')
- input_grad: float32 [4, 4096, 768], P('dp', 'seq')
- qkv_grad: float32 [768, 3, 768], P(('dp', 'seq'), None, 'mp')
- qv_bias_grad: float32 [2, 768], P(None, 'mp')
- proj_grad: float32 [768, 768], P(('dp', 'seq'), 'mp')
- proj_bias_grad: float32 [768], replicated
- first_gain_grad: float32 [768], replicated
- first_shift_grad: float32 [768], replicated
- up_grad: float32 [768, 3072], P(('dp', 'seq'), 'mp')
- up_bias_grad: float32 [3072], P('mp')
- down_grad: float32 [768, 3072], P(('dp', 'seq'), 'mp')
- down_bias_grad: float32 [768], replicated
- second_gain_grad: float32 [768], replicated
- second_shift_grad: float32 [768], replicated
The draws below stay inside these ranges and needn't reach their ends.
Inputs may be any that keep to these rules, and one draw needn't show every extreme that they name: `segments`: segment numbers start at 0 and never fall along a sequence; among the 2 sequences of each index of dp one, drawn from the seed, is a single segment, and the others have 3 boundaries.
All inputs are finite; a program needn't handle non-finite values.
Results may differ from the reference program's by a relative error of at most 0.013.
The reference program's roundings to bfloat16 on the way count: a program that leaves them out, or rounds other values in their place, can miss the bound.
Values may be sent and summed in bfloat16 or wider, within the bound.
No kernel may reach another device: no remote copies, remote signals or barrier semaphores. Data moves between devices by JAX's collectives and lax.ppermute only.
A program may use at most 448 MiB of HBM per device.

```python
import jax
import jax.numpy as jnp
from jax import lax

D = 768
HEADS = 12
FF = 3072
HEAD = 64
SEQ_DEV = 1
MICRO = 2
DOC_CUTS = 3
LENGTH = 4096
SEQS = 4


def draw_segments(key, part):
    key = jax.random.fold_in(key, 11)
    first_key, second_key = jax.random.split(key)
    row_keys = jax.random.split(first_key, SEQS)
    places = jnp.arange(LENGTH, dtype=jnp.int32)

    def one_row(row_key):
        cuts = jax.random.permutation(row_key, LENGTH - 1)[:DOC_CUTS].astype(jnp.int32) + 1
        marks = jnp.sum((places[None, :] == cuts[:, None]).astype(jnp.int32), 0)
        return jnp.cumsum(marks).astype(jnp.int32)
    ids = jax.vmap(one_row)(row_keys)
    per_group = MICRO * SEQ_DEV
    picked = jax.random.randint(second_key, (SEQS // per_group,), 0, per_group)
    rows = jnp.arange(SEQS, dtype=jnp.int32)
    whole = rows % per_group == picked[rows // per_group]
    return jnp.where(whole[:, None], 0, ids).astype(jnp.int32)


def block_levels(own_key, dims, cuts, least, high):
    factor_of = 1.0
    for dim, blocks in cuts:
        heights = jax.random.uniform(jax.random.fold_in(jax.random.fold_in(own_key, 6), dim), (blocks,), jnp.float32, least / len(cuts), high / len(cuts))
        factor_of = factor_of * jnp.repeat(jnp.exp(heights), dims[dim] // blocks).reshape((-1,) + (1,) * (len(dims) - 1 - dim))
    return factor_of


def bell_draw(stream_key, shape, scale, limit, shards=(), held_as=jnp.bfloat16):
    entries = scale * jax.random.normal(stream_key, shape, jnp.float32)
    if shards:
        entries = entries * block_levels(stream_key, shape, shards, -0.22, 0.18)
    return jnp.clip(entries, -limit, limit).astype(held_as)


def setup_inputs(seed: int = 0) -> dict:
    splits = jax.random.split(jax.random.key(seed), 16)
    return {
        "hidden_in": bell_draw(splits[0], (SEQS, LENGTH, D), 1.0, 6.0, ((0, 2), (1, 4))),
        "segments": draw_segments(jax.random.fold_in(splits[15], 71), 0),
        "cotangent": bell_draw(splits[2], (SEQS, LENGTH, D), 1.0, 6.0, ((0, 2), (1, 4))),
        "qkv_weight": bell_draw(splits[3], (D, 3, D), D ** -0.5, 0.21875, ((0, 8), (2, 4))),
        "qv_bias": bell_draw(splits[4], (2, D), 0.5, 3.0, ((1, 4),), jnp.float32),
        "proj_weight": bell_draw(splits[5], (D, D), (D // 16) ** -0.5, 0.875, ((0, 8), (1, 4))),
        "proj_bias": bell_draw(splits[6], (D,), 0.3, 2.0, (), jnp.float32),
        "first_gain": jnp.clip(1.0 + 0.1 * jax.random.normal(splits[7], (D,), jnp.float32), 0.5, 1.5),
        "first_shift": bell_draw(splits[8], (D,), 0.3, 2.0, (), jnp.float32),
        "up_weight": bell_draw(splits[9], (D, FF), D ** -0.5, 0.21875, ((0, 8), (1, 4))),
        "up_bias": bell_draw(splits[10], (FF,), 0.5, 3.0, ((0, 4),), jnp.float32),
        "down_weight": bell_draw(splits[11], (D, FF), FF ** -0.5, 0.109375, ((0, 8), (1, 4))),
        "down_bias": bell_draw(splits[12], (D,), 0.3, 2.0, (), jnp.float32),
        "second_gain": jnp.clip(1.0 + 0.1 * jax.random.normal(splits[13], (D,), jnp.float32), 0.5, 1.5),
        "second_shift": bell_draw(splits[14], (D,), 0.3, 2.0, (), jnp.float32),
    }


@jax.custom_vjp
def low(v):
    return lax.optimization_barrier(v.astype(jnp.bfloat16)).astype(jnp.float32)

@jax.custom_vjp
def low_back(v):
    return v

def low_keep(v):
    return (low(v), None)

def low_pass(kept, grad):
    return (grad,)

def back_keep(v):
    return (v, None)

def back_low(kept, grad):
    return (low(grad),)
low.defvjp(low_keep, low_pass)
low_back.defvjp(back_keep, back_low)
EPS = 1e-06
HIGH = lax.Precision.HIGHEST

def layer_norm(hidden, gain, shift):
    center = hidden - lax.optimization_barrier(jnp.mean(hidden, -1, keepdims=True))
    spread = lax.optimization_barrier(jnp.mean(center * center, -1, keepdims=True))
    return center * lax.rsqrt(spread + EPS) * gain + shift

def attend_one(pieces):
    queries, keys, values, seg = pieces
    scores = jnp.einsum('qhd,khd->hqk', queries, keys, precision=HIGH) * HEAD ** (-0.5)
    scores = low_back(scores)
    allowed = seg[:, None] == seg[None, :]
    scores = jnp.where(allowed[None], scores, -1e+30)
    top = lax.optimization_barrier(jnp.max(scores, -1, keepdims=True))
    expo = jnp.exp(scores - top)
    probs = low(expo / lax.optimization_barrier(jnp.sum(expo, -1, keepdims=True)))
    context = jnp.einsum('hqk,khd->qhd', probs, values, precision=HIGH)
    return context.reshape(context.shape[0], D)

def forward(hidden, seg, qkv_weight, qv_bias, proj_weight, proj_bias, first_gain, first_shift, up_weight, up_bias, down_weight, down_bias, second_gain, second_shift):
    group, length = (hidden.shape[0], hidden.shape[1])
    lin = jnp.einsum('gld,dce->cgle', hidden, qkv_weight, precision=HIGH)
    bias_rows = jnp.stack([qv_bias[0], jnp.zeros_like(qv_bias[0]), qv_bias[1]])
    lin = low(low_back(lin + bias_rows[:, None, None, :]))
    split = lin.reshape(3, group, length, HEADS, HEAD)
    context = lax.map(jax.checkpoint(attend_one), (split[0], split[1], split[2], seg))
    context = low(low_back(context))
    attn = low_back(jnp.einsum('gle,de->gld', context, proj_weight, precision=HIGH))
    normed = layer_norm(hidden + attn + proj_bias, first_gain, first_shift)
    pre = low_back(jnp.einsum('gld,df->glf', low(normed), up_weight, precision=HIGH) + up_bias)
    act = low(jax.nn.gelu(pre, approximate=False))
    down = low_back(jnp.einsum('glf,df->gld', act, down_weight, precision=HIGH))
    return layer_norm(normed + down + down_bias, second_gain, second_shift)

def reference(hidden_in, segments, cotangent, qkv_weight, qv_bias, proj_weight, proj_bias, first_gain, first_shift, up_weight, up_bias, down_weight, down_bias, second_gain, second_shift):
    params = tuple((p.astype(jnp.float32) for p in (qkv_weight, qv_bias, proj_weight, proj_bias, first_gain, first_shift, up_weight, up_bias, down_weight, down_bias, second_gain, second_shift)))
    groups = SEQS // 4
    xs = hidden_in.astype(jnp.float32).reshape(groups, 4, LENGTH, D)
    segs = segments.reshape(groups, 4, LENGTH)
    cots = cotangent.astype(jnp.float32).reshape(groups, 4, LENGTH, D)

    def one_group(totals, item):
        x_group, seg_group, cot_group = item

        def apply(xx, *ps):
            return forward(xx, seg_group, *ps)
        result, back_fn = jax.vjp(apply, x_group, *params)
        grads = back_fn(cot_group)
        summed = tuple((a + b for a, b in zip(totals, grads[1:])))
        return (summed, (result, grads[0]))
    start = tuple((jnp.zeros_like(p) for p in params))
    totals, (results, input_grads) = lax.scan(one_group, start, (xs, segs, cots))
    layer_out = results.reshape(SEQS, LENGTH, D).astype(jnp.bfloat16)
    input_grad = input_grads.reshape(SEQS, LENGTH, D)
    return (layer_out, input_grad, totals[0], totals[1], totals[2], totals[3], totals[4], totals[5], totals[6], totals[7], totals[8], totals[9], totals[10], totals[11])
```

```python
import functools

import jax
import jax.numpy as jnp
from jax import lax
from jax.experimental import pallas as pl
from jax.experimental.pallas import tpu as pltpu
from jax.sharding import PartitionSpec as P

HEAD = 64
EPS = 1e-06
SCALE = HEAD**-0.5
CEXP = 1.4426950408889634 * SCALE
QB = 512
KB = 512
NT = (((1,), (1,)), ((), ()))
NN = (((1,), (0,)), ((), ()))
TN = (((0,), (0,)), ((), ()))
VMEM = pl.BlockSpec(memory_space=pltpu.VMEM)
SMEM = pl.BlockSpec(memory_space=pltpu.SMEM)
PARAMS = pltpu.CompilerParams(vmem_limit_bytes=48 * 2**20)
LOW = jnp.bfloat16
FLIP = (0, 2, 1, 3)


def dot(left, right, dims):
    return lax.dot_general(left, right, dims, preferred_element_type=jnp.float32)


def visit(bounds, qi, kj, work):
    qlo, qhi, klo, khi = bounds[0, qi], bounds[1, qi], bounds[2, kj], bounds[3, kj]
    overlap = (qlo <= khi) & (klo <= qhi)
    pure = (qlo == qhi) & (klo == khi) & (qlo == klo)
    pl.when(pure)(lambda: work(False))
    pl.when(overlap & jnp.logical_not(pure))(lambda: work(True))


def fwd_body(first, bounds, segq, segk, q, k, vt, *rest):
    if first:
        top, total, acc = rest
        top[...] = jnp.full(top.shape, -1e30, jnp.float32)
        total[...] = jnp.zeros(total.shape, jnp.float32)
        acc[...] = jnp.zeros(acc.shape, jnp.float32)
    else:
        top_in, total_in, acc_in, top, total, acc = rest
        top[...] = top_in[...]
        total[...] = total_in[...]
        acc[...] = acc_in[...]

    def qstep(qi, _):
        qs = pl.ds(pl.multiple_of(qi * QB, QB), QB)

        def kstep(kj, _):
            ks = pl.ds(pl.multiple_of(kj * KB, KB), KB)

            def work(masked):
                if masked:
                    bad = segk[ks, :] != segq[0:1, qs]
                for h in range(q.shape[1] // HEAD):
                    c = slice(h * HEAD, (h + 1) * HEAD)
                    s = dot(k[ks, c], q[qs, c], NT) * CEXP
                    if masked:
                        s = jnp.where(bad, -1e30, s)
                    old = top[h : h + 1, qs]
                    new = jnp.maximum(old, jnp.max(s, 0, keepdims=True))
                    p = jnp.exp2(s - new)
                    shrink = jnp.exp2(old - new)
                    top[h : h + 1, qs] = new
                    total[h : h + 1, qs] = total[h : h + 1, qs] * shrink + jnp.sum(p, 0, keepdims=True)
                    acc[c, qs] = acc[c, qs] * shrink + dot(vt[c, ks], p.astype(LOW), NN)

            visit(bounds, qi, kj, work)
            return 0

        lax.fori_loop(0, k.shape[0] // KB, kstep, 0)
        return 0

    lax.fori_loop(0, q.shape[0] // QB, qstep, 0)


def attend(bounds, segq, segk, q, k, vt, state):
    rows, inner = q.shape
    stats = jax.ShapeDtypeStruct((8, rows), jnp.float32)
    return pl.pallas_call(
        functools.partial(fwd_body, not state),
        out_shape=(stats, stats, jax.ShapeDtypeStruct((inner, rows), jnp.float32)),
        in_specs=[SMEM] + [VMEM] * (5 + len(state)),
        out_specs=(VMEM,) * 3,
        compiler_params=PARAMS,
    )(bounds, segq, segk, q, k, vt, *state)


def bwd_body(first, bounds, segq, segk, q, do, lse, delta, k, kt, v, *rest):
    if first:
        dq, dk, dv = rest
        dq[...] = jnp.zeros(dq.shape, jnp.float32)
    else:
        dq_in, dq, dk, dv = rest
        dq[...] = dq_in[...]
    dk[...] = jnp.zeros(dk.shape, jnp.float32)
    dv[...] = jnp.zeros(dv.shape, jnp.float32)

    def kstep(kj, _):
        ks = pl.ds(pl.multiple_of(kj * KB, KB), KB)

        def qstep(qi, _):
            qs = pl.ds(pl.multiple_of(qi * QB, QB), QB)

            def work(masked):
                if masked:
                    bad = segk[ks, :] != segq[0:1, qs]
                for h in range(q.shape[1] // HEAD):
                    c = slice(h * HEAD, (h + 1) * HEAD)
                    qh = q[qs, c]
                    dh = do[qs, c]
                    s = dot(k[ks, c], qh, NT) * CEXP - lse[h : h + 1, qs]
                    if masked:
                        s = jnp.where(bad, -1e30, s)
                    p = jnp.exp2(s)
                    dp = dot(v[ks, c], dh, NT)
                    ds = (p * (dp - delta[h : h + 1, qs])).astype(LOW)
                    dv[ks, c] += dot(p.astype(LOW), dh, NN)
                    dk[ks, c] += dot(ds, qh, NN)
                    dq[c, qs] += dot(kt[c, ks], ds, NN)

            visit(bounds, qi, kj, work)
            return 0

        lax.fori_loop(0, q.shape[0] // QB, qstep, 0)
        return 0

    lax.fori_loop(0, k.shape[0] // KB, kstep, 0)


def attend_back(bounds, segq, segk, q, do, lse, delta, k, kt, v, state):
    rows, inner = q.shape
    by_key = jax.ShapeDtypeStruct(k.shape, jnp.float32)
    return pl.pallas_call(
        functools.partial(bwd_body, not state),
        out_shape=(jax.ShapeDtypeStruct((inner, rows), jnp.float32), by_key, by_key),
        in_specs=[SMEM] + [VMEM] * (9 + len(state)),
        out_specs=(VMEM,) * 3,
        compiler_params=PARAMS,
    )(bounds, segq, segk, q, do, lse, delta, k, kt, v, *state)


def normalize(hidden):
    center = hidden - jnp.mean(hidden, -1, keepdims=True)
    spread = jnp.mean(center * center, -1, keepdims=True)
    return center * lax.rsqrt(spread + EPS)


def flip(value, axis, bit):
    size = lax.axis_size(axis)
    return lax.ppermute(value, axis, [(i, i ^ bit) for i in range(size)])


def onward(value):
    size = lax.axis_size("seq")
    return lax.ppermute(value, "seq", [(i, (i + 1) % size) for i in range(size)])


def low_sum(left, right):
    return (left.astype(jnp.float32) + right.astype(jnp.float32)).astype(LOW)


def shards(
    hidden_in,
    segments,
    cotangent,
    qkv_weight,
    qv_bias,
    proj_weight,
    proj_bias,
    first_gain,
    first_shift,
    up_weight,
    up_bias,
    down_weight,
    down_bias,
    second_gain,
    second_shift,
):
    batch, local_len, width = hidden_in.shape
    inner = qkv_weight.shape[2]
    heads = inner // HEAD
    units = up_weight.shape[1]
    n_dp, n_seq, n_mp = lax.axis_size("dp"), lax.axis_size("seq"), lax.axis_size("mp")
    assert n_mp == 4
    d_at, s_at, m_at = lax.axis_index("dp"), lax.axis_index("seq"), lax.axis_index("mp")
    chunk_at = (m_at % 2) * 2 + m_at // 2
    share = local_len // n_mp
    own_rows = batch * share
    shard_rows = qkv_weight.shape[0]
    halves = n_dp == 2

    def place(pieces, positions):
        rows = pieces[0].shape[0]
        whole = jnp.zeros((rows * len(pieces),) + pieces[0].shape[1:], pieces[0].dtype)
        for piece, position in zip(pieces, positions):
            whole = lax.dynamic_update_slice_in_dim(whole, piece, position * rows, 0)
        return whole

    def relative(rows):
        return jnp.concatenate(
            [lax.dynamic_slice_in_dim(rows, (chunk_at ^ i) * share, share, 0) for i in range(4)], 0
        )

    def own(rows):
        return lax.dynamic_slice_in_dim(rows, chunk_at * share, share, 1).reshape(own_rows, -1)

    def swapped(rows):
        if not halves:
            return rows
        first, second = jnp.split(rows, 2, -1)
        return jnp.where(d_at == 1, jnp.concatenate([second, first], -1), rows)

    def share_over_mp(piece):
        pair = jnp.concatenate([piece, flip(piece, "mp", 2)], 0)
        return jnp.concatenate([pair, flip(pair, "mp", 1)], 0)

    def sum_over_mp(rows):
        half = rows.shape[0] // 2
        pair = low_sum(rows[:half], flip(rows[half:], "mp", 1))
        quarter = half // 2
        return pair[:quarter].astype(jnp.float32) + flip(pair[quarter:], "mp", 2).astype(jnp.float32)

    flat_qkv = qkv_weight.reshape(shard_rows, 3 * inner)
    if halves:
        pieces, positions = [flat_qkv], [d_at * n_seq + s_at]
        for dy in range(2):
            for dz in range(n_seq):
                if dy or dz:
                    pairs = [
                        (y * n_seq + z, (y ^ dy) * n_seq + (z + dz) % n_seq)
                        for y in range(2)
                        for z in range(n_seq)
                    ]
                    pieces.append(lax.ppermute(flat_qkv, ("dp", "seq"), pairs))
                    positions.append((d_at ^ dy) * n_seq + (s_at - dz) % n_seq)
        full_qkv = place(pieces, positions)
    else:
        full_qkv = lax.all_gather(flat_qkv, ("dp", "seq"), axis=0, tiled=True)
    weight_q, weight_k, weight_v = (full_qkv[:, i * inner : (i + 1) * inner] for i in range(3))

    seg_now = segments.astype(jnp.float32)
    seg_whole = [lax.all_gather(seg_now.astype(LOW), "seq", axis=0, tiled=False)]
    hidden_blocks = [[relative(hidden_in[b]) for b in range(batch)]]
    seg_blocks = [[relative(seg_now[b]) for b in range(batch)]]
    travel = [hidden_blocks[0][b][:share] for b in range(batch)]
    for t in range(1, n_seq):
        travel = [onward(piece) for piece in travel]
        hidden_blocks.append([share_over_mp(piece) for piece in travel])
        source = (s_at - t) % n_seq
        seg_there = lax.dynamic_index_in_dim(seg_whole[0], source, 0, keepdims=False)
        seg_blocks.append([relative(seg_there[b].astype(jnp.float32)) for b in range(batch)])

    def limits(queries, keys):
        parts_q, parts_k = queries.reshape(-1, QB), keys.reshape(-1, KB)
        return jnp.stack(
            [jnp.min(parts_q, 1), jnp.max(parts_q, 1), jnp.min(parts_k, 1), jnp.max(parts_k, 1)]
        ).astype(jnp.int32)

    bounds = [[limits(seg_blocks[0][b], seg_blocks[t][b]) for b in range(batch)] for t in range(n_seq)]
    seg_row = [seg_blocks[0][b][None, :] for b in range(batch)]
    seg_col = [[seg_blocks[t][b][:, None] for b in range(batch)] for t in range(n_seq)]

    queries = [(dot(hidden_blocks[0][b], weight_q, NN) + qv_bias[0]).astype(LOW) for b in range(batch)]
    keys, keys_t, values = [], [], []
    state = [()] * batch
    for t in range(n_seq):
        keys.append([])
        keys_t.append([])
        values.append([])
        for b in range(batch):
            key = dot(hidden_blocks[t][b], weight_k, NN).astype(LOW)
            value = (dot(hidden_blocks[t][b], weight_v, NN) + qv_bias[1]).astype(LOW)
            keys[t].append(key)
            keys_t[t].append(key.T)
            values[t].append(value)
            state[b] = attend(
                bounds[t][b], seg_row[b], seg_col[t][b], queries[b], key, value.T, tuple(state[b])
            )
    lse, context_full, context_low = [], [], []
    for b in range(batch):
        top, total, acc = state[b]
        lse.append(top + jnp.log2(jnp.where(total > 0, total, 1.0)))
        spread = jnp.broadcast_to(total[:heads, None, :], (heads, HEAD, local_len)).reshape(inner, -1)
        context_full.append((acc / spread).T)
        context_low.append(context_full[b].astype(LOW))
    context_sent = [
        jnp.concatenate([context_low[b][i * share : (i + 1) * share] for b in range(batch)], 0)
        for i in range(4)
    ]
    context = [context_sent[0]] + [flip(context_sent[i], "mp", FLIP[i]) for i in range(1, 4)]

    shard = jnp.concatenate([up_weight, down_weight, proj_weight], 1)
    pieces, positions = [shard], [s_at]
    for t in range(1, n_seq):
        pieces.append(onward(pieces[-1]))
        positions.append((s_at - t) % n_seq)
    seq_whole = place(pieces, positions)

    def over_dp(block):
        if halves:
            return jnp.concatenate([block, flip(block, "dp", 1)], 0)
        gathered = lax.all_gather(block, "dp", axis=0, tiled=True)
        return gathered

    near = over_dp(seq_whole)
    far = over_dp(flip(seq_whole, "mp", 2))
    blocks = [near, far, flip(near, "mp", 1), flip(far, "mp", 1)]
    ups = [block[:, :units] for block in blocks]
    downs = [block[:, units : 2 * units] for block in blocks]
    projs = [block[:, 2 * units :] for block in blocks]
    bias_far = flip(up_bias, "mp", 2)
    biases = [up_bias, bias_far, flip(up_bias, "mp", 1), flip(bias_far, "mp", 1)]

    attn = sum(dot(context[i], projs[i], NT) for i in range(4))
    hidden_own = own(hidden_in).astype(jnp.float32)
    first_in = hidden_own + swapped(attn) + proj_bias
    unit_one, first_back = jax.vjp(normalize, first_in)
    normed = unit_one * first_gain + first_shift
    normed_low = swapped(normed.astype(LOW))
    acts, slopes = [], []
    down = 0.0
    for i in range(4):
        pre = dot(normed_low, ups[i], NN) + biases[i]
        gate = 0.5 * (1.0 + lax.erf(pre * 0.7071067811865476))
        acts.append((pre * gate).astype(LOW))
        slopes.append(gate + pre * (0.3989422804014327 * jnp.exp(-0.5 * pre * pre)))
        down = down + dot(acts[i], downs[i], NT)
    second_in = normed + swapped(down) + down_bias
    unit_two, second_back = jax.vjp(normalize, second_in)
    out_own = (unit_two * second_gain + second_shift).astype(LOW)
    cot = own(cotangent).astype(jnp.float32)
    grad_second = second_back(cot * second_gain)[0]
    sums = [
        jnp.sum(grad_second, 0),
        jnp.sum(cot * unit_two, 0),
        jnp.sum(cot, 0),
    ]
    down_low = swapped(grad_second.astype(LOW))
    grads_up, grads_down, bias_sums = [], [], []
    normed_part = 0.0
    for i in range(4):
        pre_low = (dot(down_low, downs[i], NN) * slopes[i]).astype(LOW)
        bias_sums.append(jnp.sum(pre_low.astype(jnp.float32), 0))
        normed_part = normed_part + dot(pre_low, ups[i], NT)
        grads_up.append(dot(normed_low, pre_low, TN).astype(LOW))
        grads_down.append(dot(down_low, acts[i], TN).astype(LOW))
    grad_normed = grad_second + swapped(normed_part)
    grad_first = first_back(grad_normed * first_gain)[0]
    sums += [
        jnp.sum(grad_first, 0),
        jnp.sum(grad_normed * unit_one, 0),
        jnp.sum(grad_normed, 0),
    ]
    attn_low = swapped(grad_first.astype(LOW))
    grads_proj = [dot(attn_low, context[i], TN).astype(LOW) for i in range(4)]
    back = [dot(attn_low, projs[i], NN).astype(LOW) for i in range(4)]
    back = [back[0]] + [flip(back[i], "mp", FLIP[i]) for i in range(1, 4)]
    grad_context = [
        jnp.concatenate([back[i][b * share : (b + 1) * share] for i in range(4)], 0)
        for b in range(batch)
    ]

    def spread_rows(piece):
        parts = share_over_mp(piece)
        rows = piece.shape[0]
        return [parts[i * rows : (i + 1) * rows] for i in range(4)]

    def assemble(parts, dtype):
        whole = jnp.zeros((batch, local_len, width), dtype)
        for i in range(4):
            whole = lax.dynamic_update_slice_in_dim(
                whole, parts[i].reshape(batch, share, width).astype(dtype), (chunk_at ^ i) * share, 1
            )
        return whole

    layer_out = assemble(spread_rows(out_own), LOW)

    def owned_sum(grads):
        near = low_sum(grads[0], flip(grads[2], "mp", 1))
        far = low_sum(grads[1], flip(grads[3], "mp", 1))
        if halves:
            rows = near.shape[0] // 2
            near = low_sum(near[:rows], flip(near[rows:], "dp", 1))
            far = low_sum(far[:rows], flip(far[rows:], "dp", 1))
        else:
            near = lax.psum_scatter(near, "dp", scatter_dimension=0, tiled=True)
            far = lax.psum_scatter(far, "dp", scatter_dimension=0, tiled=True)
        return ring_sum(low_sum(near, flip(far, "mp", 2)))

    def ring_sum(rows):
        height = rows.shape[0] // n_seq
        total = None
        for t in range(1, n_seq + 1):
            part = lax.dynamic_slice_in_dim(rows, ((s_at - t) % n_seq) * height, height, 0)
            part = part.astype(jnp.float32)
            if total is not None:
                part = part + onward(total).astype(jnp.float32)
            total = part.astype(LOW)
        return part

    up_owned = owned_sum(grads_up)
    down_owned = owned_sum(grads_down)
    proj_owned = owned_sum(grads_proj)

    common = jnp.stack(sums)
    split = jnp.stack(bias_sums)
    small = jnp.concatenate([common.reshape(-1), split.reshape(-1)])
    cut = common.size
    far_small = flip(small, "mp", 2)
    common = small[:cut] + far_small[:cut]
    split = small[cut:].reshape(4, units)
    far_split = far_small[cut:].reshape(4, units)
    near_bias, next_bias = split[0] + far_split[1], split[2] + far_split[3]
    small = jnp.concatenate([common, next_bias])
    far_small = flip(small, "mp", 1)
    small = jnp.concatenate([common + far_small[:cut], near_bias + far_small[cut:]])

    def over_groups(value):
        for axis, size in (("dp", n_dp), ("seq", n_seq)):
            bit = 1
            while bit < size:
                value = value + flip(value, axis, bit)
                bit *= 2
        return value

    small = over_groups(small)
    norm_sums = small[:cut].reshape(-1, width)
    up_bias_grad = small[cut:]

    delta = []
    for b in range(batch):
        product = context_full[b] * grad_context[b].astype(jnp.float32)
        per_head = jnp.sum(product.reshape(local_len, heads, HEAD), -1)
        delta.append(jnp.pad(per_head.T, ((0, 8 - heads), (0, 0))))
    state = [()] * batch
    passing = [None] * batch
    grad_k = grad_v = grad_q = 0.0
    bias_q = bias_v = 0.0
    input_rows = [None] * batch
    for t in list(range(1, n_seq)) + [0]:
        for b in range(batch):
            dq, dk, dv = attend_back(
                bounds[t][b], seg_row[b], seg_col[t][b], queries[b], grad_context[b], lse[b], delta[b],
                keys[t][b], keys_t[t][b], values[t][b], tuple(state[b]),
            )
            state[b] = (dq,)
            bias_v = bias_v + jnp.sum(dv, 0)
            dk_low, dv_low = (dk * SCALE).astype(LOW), dv.astype(LOW)
            grad_k = grad_k + dot(hidden_blocks[t][b], dk_low, TN)
            grad_v = grad_v + dot(hidden_blocks[t][b], dv_low, TN)
            rows = dot(dk_low, weight_k, NT) + dot(dv_low, weight_v, NT)
            if t == 0:
                dq_low = (dq.T * SCALE).astype(LOW)
                bias_q = bias_q + jnp.sum(dq, 1) * SCALE
                grad_q = grad_q + dot(hidden_blocks[0][b], dq_low, TN)
                rows = rows + dot(dq_low, weight_q, NT)
            rows = sum_over_mp(rows.astype(LOW))
            if passing[b] is not None:
                rows = rows + onward(passing[b]).astype(jnp.float32)
            passing[b] = rows.astype(LOW)
            input_rows[b] = rows
    input_own = (grad_first + jnp.concatenate(input_rows, 0)).astype(LOW)
    input_grad = assemble(spread_rows(input_own), jnp.float32)
    grad_qkv = jnp.concatenate([grad_q, grad_k, grad_v], 1).astype(LOW)
    if halves:
        rows = width // 2
        mine = lax.dynamic_slice_in_dim(grad_qkv, d_at * rows, rows, 0)
        theirs = lax.dynamic_slice_in_dim(grad_qkv, (1 - d_at) * rows, rows, 0)
        grad_qkv = low_sum(mine, flip(theirs, "dp", 1))
    else:
        grad_qkv = lax.psum_scatter(grad_qkv, "dp", scatter_dimension=0, tiled=True)
    qkv_owned = ring_sum(grad_qkv).reshape(shard_rows, 3, inner)
    qv_bias_grad = over_groups(jnp.stack([bias_q, bias_v]))
    return (
        layer_out,
        input_grad,
        qkv_owned,
        qv_bias_grad,
        proj_owned,
        norm_sums[3],
        norm_sums[4],
        norm_sums[5],
        up_owned,
        up_bias_grad,
        down_owned,
        norm_sums[0],
        norm_sums[1],
        norm_sums[2],
    )


def solution(mesh):
    in_specs = (
        P("dp", "seq", None),
        P("dp", "seq"),
        P("dp", "seq", None),
        P(("dp", "seq"), None, "mp"),
        P(None, "mp"),
        P(("dp", "seq"), "mp"),
        P(),
        P(),
        P(),
        P(("dp", "seq"), "mp"),
        P("mp"),
        P(("dp", "seq"), "mp"),
        P(),
        P(),
        P(),
    )
    out_specs = (
        P("dp", "seq", None),
        P("dp", "seq", None),
        P(("dp", "seq"), None, "mp"),
        P(None, "mp"),
        P(("dp", "seq"), "mp"),
        P(),
        P(),
        P(),
        P(("dp", "seq"), "mp"),
        P("mp"),
        P(("dp", "seq"), "mp"),
        P(),
        P(),
        P(),
    )
    return jax.shard_map(shards, mesh=mesh, in_specs=in_specs, out_specs=out_specs, check_vma=False)
```

```python
import functools

import jax
import jax.numpy as jnp
from jax import lax
from jax.experimental import pallas as pl
from jax.experimental.pallas import tpu as pltpu
from jax.sharding import PartitionSpec as P

HEAD = 64
EPS = 1e-06
SCALE = HEAD**-0.5
LOG2E = 1.4426950408889634
CEXP = LOG2E * SCALE
QB = 512
KB = 512
NT = (((1,), (1,)), ((), ()))
NN = (((1,), (0,)), ((), ()))
VMEM = pl.BlockSpec(memory_space=pltpu.VMEM)
SMEM = pl.BlockSpec(memory_space=pltpu.SMEM)
LOW = jnp.bfloat16
F32 = jnp.float32
FLIP = (0, 2, 1, 3)


def dot(left, right, dims):
    return lax.dot_general(left, right, dims, preferred_element_type=F32)


def struct(shape, dtype):
    return jax.ShapeDtypeStruct(shape, dtype)


def call(body, ins, outs, scratch, mib, scalars=1):
    return pl.pallas_call(
        body,
        out_shape=tuple(outs),
        in_specs=[SMEM] * scalars + [VMEM] * (len(ins) - scalars),
        out_specs=(VMEM,) * len(outs),
        scratch_shapes=scratch,
        compiler_params=pltpu.CompilerParams(vmem_limit_bytes=mib * 2**20),
    )(*ins)


def visit(bounds, qi, kj, work):
    qlo, qhi, klo, khi = bounds[0, qi], bounds[1, qi], bounds[2, kj], bounds[3, kj]
    overlap = (qlo <= khi) & (klo <= qhi)
    pure = (qlo == qhi) & (klo == khi) & (qlo == klo)
    pl.when(pure)(lambda: work(False))
    pl.when(overlap & jnp.logical_not(pure))(lambda: work(True))


def fill(target, pieces):
    rows = pieces[0].shape[0]
    for i, piece in enumerate(pieces):
        target[i * rows : (i + 1) * rows, :] = piece[...]


def segment_column(target, segk):
    target[...] = jnp.broadcast_to(segk[...], (128, segk.shape[1])).T


def fwd_body(first, last, bounds, segq, segk, *refs):
    refs = list(refs)
    pieces = [refs.pop(0) for _ in range(4)]
    wkv, vbias = refs.pop(0), refs.pop(0)
    if first:
        wq, qbias = refs.pop(0), refs.pop(0)
        before = None
    else:
        q = refs.pop(0)
        before = [refs.pop(0) for _ in range(3)]
    kv = refs.pop(0)
    if first:
        q = refs.pop(0)
    if last:
        contexts = [refs.pop(0) for _ in range(4)]
        out_t, lse = refs.pop(0), refs.pop(0)
    top, total, acc = refs.pop(0), refs.pop(0), refs.pop(0)
    hidden, vt, segc = refs
    inner = q.shape[1]
    fill(hidden, pieces)
    segment_column(segc, segk)
    value = dot(hidden[...], wkv[...], NN)
    kv[:, :inner] = value[:, :inner].astype(LOW)
    value = value[:, inner:] + vbias[...]
    kv[:, inner:] = value.astype(LOW)
    vt[...] = value.T.astype(LOW)
    if first:
        q[...] = (dot(hidden[...], wq[...], NN) + qbias[...]).astype(LOW)
        top[...] = jnp.full(top.shape, -1e30, F32)
        total[...] = jnp.zeros(total.shape, F32)
        acc[...] = jnp.zeros(acc.shape, F32)
    else:
        top[...], total[...], acc[...] = (ref[...] for ref in before)

    def qstep(qi, _):
        qs = pl.ds(pl.multiple_of(qi * QB, QB), QB)

        def kstep(kj, _):
            ks = pl.ds(pl.multiple_of(kj * KB, KB), KB)

            def work(masked):
                if masked:
                    bad = segc[ks, 0:1] != segq[0:1, qs]
                for h in range(inner // HEAD):
                    c = slice(h * HEAD, (h + 1) * HEAD)
                    s = dot(kv[ks, c], q[qs, c], NT) * CEXP
                    if masked:
                        s = jnp.where(bad, -1e30, s)
                    old = top[h : h + 1, qs]
                    new = jnp.maximum(old, jnp.max(s, 0, keepdims=True))
                    p = jnp.exp2(s - new)
                    shrink = jnp.exp2(old - new)
                    top[h : h + 1, qs] = new
                    total[h : h + 1, qs] = total[h : h + 1, qs] * shrink + jnp.sum(p, 0, keepdims=True)
                    acc[c, qs] = acc[c, qs] * shrink + dot(vt[c, ks], p.astype(LOW), NN)

            visit(bounds, qi, kj, work)
            return 0

        lax.fori_loop(0, kv.shape[0] // KB, kstep, 0)
        return 0

    lax.fori_loop(0, q.shape[0] // QB, qstep, 0)
    if last:
        for h in range(inner // HEAD):
            c = slice(h * HEAD, (h + 1) * HEAD)
            out_t[c, :] = acc[c, :] / total[h : h + 1, :]
            lse[h : h + 1, :] = top[h : h + 1, :] + jnp.log(total[h : h + 1, :]) * LOG2E
        natural = out_t[...].T.astype(LOW)
        rows = contexts[0].shape[0]
        for i in range(4):
            contexts[i][...] = natural[i * rows : (i + 1) * rows, :]


def attend(first, last, bounds, segq, segk, pieces, wkv, vbias, more):
    rows = 4 * pieces[0].shape[0]
    width, inner = wkv.shape[0], wkv.shape[1] // 2
    stats = [((8, rows), F32), ((8, rows), F32), ((inner, rows), F32)]
    outs = [struct((rows, 2 * inner), LOW)]
    if first:
        outs.append(struct((rows, inner), LOW))
    if last:
        outs += [struct((rows // 4, inner), LOW)] * 4 + [struct((inner, rows), F32), struct((8, rows), F32)]
    else:
        outs += [struct(*item) for item in stats]
    scratch = [pltpu.VMEM(*item) for item in stats] if last else []
    scratch += [pltpu.VMEM((rows, width), LOW), pltpu.VMEM((inner, rows), LOW), pltpu.VMEM((rows, 128), F32)]
    ins = [bounds, segq, segk, *pieces, wkv, vbias, *more]
    return call(functools.partial(fwd_body, first, last), ins, outs, scratch, 24)


def bwd_body(first, last, add, bounds, segq, segk, *refs):
    refs = list(refs)
    pieces = [refs.pop(0) for _ in range(4)]
    back = [refs.pop(0) for _ in range(4)]
    wkv, q, kv, lse, extra = (refs.pop(0) for _ in range(5))
    if not first:
        dq_before = refs.pop(0)
    if add:
        gkv_before = refs.pop(0)
    if last:
        wq = refs.pop(0)
    keep, send, gkv, vsum = (refs.pop(0) for _ in range(4))
    if first:
        delta = refs.pop(0)
    else:
        delta = extra
    if last:
        gq, qsum = refs.pop(0), refs.pop(0)
    dq = refs.pop(0)
    hidden, do, kt, segc, dk, dv, dkv = refs
    inner = q.shape[1]
    fill(hidden, pieces)
    fill(do, back)
    segment_column(segc, segk)
    kt[...] = kv[:, :inner].astype(F32).T.astype(LOW)
    if first:
        product = do[...].astype(F32).T * extra[...]
        delta[...] = jnp.zeros(delta.shape, F32)
        for h in range(inner // HEAD):
            delta[h : h + 1, :] = jnp.sum(product[h * HEAD : (h + 1) * HEAD, :], 0, keepdims=True)
        dq[...] = jnp.zeros(dq.shape, F32)
    else:
        dq[...] = dq_before[...]
    dk[...] = jnp.zeros(dk.shape, F32)
    dv[...] = jnp.zeros(dv.shape, F32)

    def kstep(kj, _):
        ks = pl.ds(pl.multiple_of(kj * KB, KB), KB)

        def qstep(qi, _):
            qs = pl.ds(pl.multiple_of(qi * QB, QB), QB)

            def work(masked):
                if masked:
                    bad = segc[ks, 0:1] != segq[0:1, qs]
                for h in range(inner // HEAD):
                    c = slice(h * HEAD, (h + 1) * HEAD)
                    cv = slice(inner + h * HEAD, inner + (h + 1) * HEAD)
                    qh = q[qs, c]
                    dh = do[qs, c]
                    s = dot(kv[ks, c], qh, NT) * CEXP - lse[h : h + 1, qs]
                    if masked:
                        s = jnp.where(bad, -1e30, s)
                    p = jnp.exp2(s)
                    dp = dot(kv[ks, cv], dh, NT)
                    ds = (p * (dp - delta[h : h + 1, qs])).astype(LOW)
                    dv[ks, c] += dot(p.astype(LOW), dh, NN)
                    dk[ks, c] += dot(ds, qh, NN)
                    dq[c, qs] += dot(kt[c, ks], ds, NN)

            visit(bounds, qi, kj, work)
            return 0

        lax.fori_loop(0, q.shape[0] // QB, qstep, 0)
        return 0

    lax.fori_loop(0, kv.shape[0] // KB, kstep, 0)
    dkv[:, :inner] = (dk[...] * SCALE).astype(LOW)
    dkv[:, inner:] = dv[...].astype(LOW)
    vsum[...] = jnp.broadcast_to(jnp.sum(dv[...], 0, keepdims=True), vsum.shape)
    half = keep.shape[0]
    if last:
        dq_low = (dq[...] * SCALE).T
        qsum[...] = jnp.broadcast_to(jnp.sum(dq_low, 0, keepdims=True), qsum.shape)
        dq_low = dq_low.astype(LOW)
        gq[...] = dot((dq[...] * SCALE).astype(LOW), hidden[...], NN)
    for part, out in ((slice(0, half), keep), (slice(half, 2 * half), send)):
        value = dot(dkv[part, :], wkv[...], NT)
        if last:
            value = value + dot(dq_low[part, :], wq[...], NT)
        out[...] = value.astype(LOW)
    parts = [(dk[...] * SCALE).T.astype(LOW), dv[...].T.astype(LOW)]
    for i in range(2):
        rows = slice(i * inner, (i + 1) * inner)
        value = dot(parts[i], hidden[...], NN)
        gkv[rows, :] = gkv_before[rows, :] + value if add else value


def attend_back(first, last, bounds, segq, segk, pieces, back, wkv, q, kv, lse, extra, dq, gkv, wq):
    rows, inner = q.shape
    width = wkv.shape[0]
    outs = [struct((rows // 2, width), LOW)] * 2 + [struct((2 * inner, width), F32), struct((8, inner), F32)]
    if first:
        outs.append(struct((8, rows), F32))
    if last:
        outs += [struct((inner, width), F32), struct((8, inner), F32)]
    scratch = []
    if last:
        scratch.append(pltpu.VMEM((inner, rows), F32))
    else:
        outs.append(struct((inner, rows), F32))
    scratch += [
        pltpu.VMEM((rows, width), LOW),
        pltpu.VMEM((rows, inner), LOW),
        pltpu.VMEM((inner, rows), LOW),
        pltpu.VMEM((rows, 128), F32),
        pltpu.VMEM((rows, inner), F32),
        pltpu.VMEM((rows, inner), F32),
        pltpu.VMEM((rows, 2 * inner), LOW),
    ]
    ins = [bounds, segq, segk, *pieces, *back, wkv, q, kv, lse, extra]
    ins += [] if first else [dq]
    ins += [] if gkv is None else [gkv]
    ins += [wq] if last else []
    return call(functools.partial(bwd_body, first, last, gkv is not None), ins, outs, scratch, 28)


def rows_body(halves, batch, flag, *refs):
    refs = list(refs)
    take = lambda count: [refs.pop(0) for _ in range(count)]
    ctx_in = take(4 * batch)
    hidden, cot, vec, bias = take(4)
    low_w, high_w = take(4), take(4)
    out_low, grad_first, sums, bias_sums = take(4)
    back = take(4 * batch)
    acts, pres, ctxs = take(4), take(4), take(4)
    nl_t, dl_t, al_t = take(3)
    slopes = take(4)
    width = hidden.shape[1]
    half = width // 2
    units = (low_w[0].shape[1] - ctxs[0].shape[1]) // 2
    up, down, proj = slice(0, units), slice(units, 2 * units), slice(2 * units, low_w[0].shape[1])

    def swapped(value):
        if not halves:
            return value
        turned = jnp.concatenate([value[:, half:], value[:, :half]], 1)
        return jnp.where(flag[0] == 1, turned, value)

    def into(value, r, cols):
        return dot(value[:, :half], low_w[r][:, cols], NN) + dot(value[:, half:], high_w[r][:, cols], NN)

    def out_of(value, r, cols):
        return jnp.concatenate([dot(value, low_w[r][:, cols], NT), dot(value, high_w[r][:, cols], NT)], 1)

    def norm(value):
        center = value - jnp.mean(value, -1, keepdims=True)
        inverse = lax.rsqrt(jnp.mean(center * center, -1, keepdims=True) + EPS)
        return center * inverse, inverse

    def norm_back(grad, unit, inverse):
        shared = jnp.mean(grad, -1, keepdims=True)
        return inverse * (grad - shared - unit * jnp.mean(grad * unit, -1, keepdims=True))

    attn = None
    for r in range(4):
        fill(ctxs[r], [ctx_in[b * 4 + r] for b in range(batch)])
        part = out_of(ctxs[r][...], r, proj)
        attn = part if attn is None else attn + part
    unit_one, inverse_one = norm(hidden[...].astype(F32) + swapped(attn) + vec[0:1, :])
    normed = unit_one * vec[1:2, :] + vec[2:3, :]
    normed_sw = swapped(normed)
    nl_t[...] = normed_sw.T.astype(LOW)
    normed_low = normed_sw.astype(LOW)
    total = None
    for r in range(4):
        pre = into(normed_low, r, up) + bias[r : r + 1, :]
        gate = 0.5 + 0.5 * lax.erf(pre * 0.7071067811865476)
        acts[r][...] = (pre * gate).astype(LOW)
        slopes[r][...] = gate + pre * (0.3989422804014327 * jnp.exp(-0.5 * pre * pre))
        part = out_of(acts[r][...], r, down)
        total = part if total is None else total + part
    unit_two, inverse_two = norm(normed + swapped(total) + vec[3:4, :])
    out_low[...] = (unit_two * vec[4:5, :] + vec[5:6, :]).astype(LOW)
    cotangent = cot[...].astype(F32)
    grad_second = norm_back(cotangent * vec[4:5, :], unit_two, inverse_two)
    sums[...] = jnp.zeros(sums.shape, F32)
    sums[0:1, :] = jnp.sum(grad_second, 0, keepdims=True)
    sums[1:2, :] = jnp.sum(cotangent * unit_two, 0, keepdims=True)
    sums[2:3, :] = jnp.sum(cotangent, 0, keepdims=True)
    second_sw = swapped(grad_second)
    dl_t[...] = second_sw.T.astype(LOW)
    down_low = second_sw.astype(LOW)
    total = None
    for r in range(4):
        pre_low = (into(down_low, r, down) * slopes[r][...]).astype(LOW)
        pres[r][...] = pre_low
        bias_sums[r : r + 1, :] = jnp.sum(pre_low.astype(F32), 0, keepdims=True)
        part = out_of(pre_low, r, up)
        total = part if total is None else total + part
    grad_normed = grad_second + swapped(total)
    first = norm_back(grad_normed * vec[1:2, :], unit_one, inverse_one)
    grad_first[...] = first
    sums[3:4, :] = jnp.sum(first, 0, keepdims=True)
    sums[4:5, :] = jnp.sum(grad_normed * unit_one, 0, keepdims=True)
    sums[5:6, :] = jnp.sum(grad_normed, 0, keepdims=True)
    first_sw = swapped(first)
    al_t[...] = first_sw.T.astype(LOW)
    attn_low = first_sw.astype(LOW)
    share = back[0].shape[0]
    for r in range(4):
        value = into(attn_low, r, proj).astype(LOW)
        for b in range(batch):
            back[b * 4 + r][...] = value[b * share : (b + 1) * share, :]


def own_rows_pass(halves, batch, flag, ctx, hidden, cot, vec, bias, low_w, high_w):
    rows, width = hidden.shape
    share, inner = ctx[0].shape
    units = bias.shape[1]
    outs = [struct((rows, width), LOW), struct((rows, width), F32), struct((8, width), F32), struct((4, units), F32)]
    outs += [struct((share, inner), LOW)] * (4 * batch)
    outs += [struct((rows, units), LOW)] * 8 + [struct((rows, inner), LOW)] * 4
    outs += [struct((width, rows), LOW)] * 3
    ins = [flag, *ctx, hidden, cot, vec, bias, *low_w, *high_w]
    scratch = [pltpu.VMEM((rows, units), F32)] * 4
    return call(functools.partial(rows_body, halves, batch), ins, outs, scratch, 40)


def grads_body(nl_t, dl_t, al_t, pre, act, ctx, out):
    units = act.shape[1]
    out[:, :units] = dot(nl_t[...], pre[...], NN).astype(LOW)
    out[:, units : 2 * units] = dot(dl_t[...], act[...], NN).astype(LOW)
    out[:, 2 * units :] = dot(al_t[...], ctx[...], NN).astype(LOW)


def weight_grads(nl_t, dl_t, al_t, pre, act, ctx):
    shape = (nl_t.shape[0], 2 * act.shape[1] + ctx.shape[1])
    return call(grads_body, [nl_t, dl_t, al_t, pre, act, ctx], [struct(shape, LOW)], [], 20, 0)[0]


def flip(value, axis, bit):
    size = lax.axis_size(axis)
    return lax.ppermute(value, axis, [(i, i ^ bit) for i in range(size)])


def onward(value, step=1):
    size = lax.axis_size("seq")
    return lax.ppermute(value, "seq", [(i, (i + step) % size) for i in range(size)])


def after(value, *others):
    return lax.optimization_barrier((value,) + others)[0]


def low_sum(left, right):
    return (left.astype(F32) + right.astype(F32)).astype(LOW)


def shards(
    hidden_in,
    segments,
    cotangent,
    qkv_weight,
    qv_bias,
    proj_weight,
    proj_bias,
    first_gain,
    first_shift,
    up_weight,
    up_bias,
    down_weight,
    down_bias,
    second_gain,
    second_shift,
):
    batch, local_len, width = hidden_in.shape
    inner = qkv_weight.shape[2]
    n_dp, n_seq, n_mp = lax.axis_size("dp"), lax.axis_size("seq"), lax.axis_size("mp")
    assert n_mp == 4
    d_at, s_at, m_at = lax.axis_index("dp"), lax.axis_index("seq"), lax.axis_index("mp")
    chunk_at = (m_at % 2) * 2 + m_at // 2
    share = local_len // n_mp
    shard_rows = qkv_weight.shape[0]
    halves = n_dp == 2

    def place(pieces, positions):
        whole = jnp.zeros((len(pieces),) + pieces[0].shape, pieces[0].dtype)
        for piece, position in zip(pieces, positions):
            whole = lax.dynamic_update_index_in_dim(whole, piece, position, 0)
        return whole.reshape((-1,) + pieces[0].shape[1:])

    def chunk(rows, i):
        parts = rows.reshape((4, share) + rows.shape[1:])
        return lax.dynamic_index_in_dim(parts, chunk_at ^ i, 0, keepdims=False)

    def own(rows):
        return jnp.concatenate([chunk(rows[b], 0) for b in range(batch)], 0)

    flat_qkv = qkv_weight.reshape(shard_rows, 3 * inner)
    if halves:
        pieces, positions = [flat_qkv], [d_at * n_seq + s_at]
        for dy in range(2):
            for dz in range(n_seq):
                if dy or dz:
                    pairs = [
                        (y * n_seq + z, (y ^ dy) * n_seq + (z + dz) % n_seq)
                        for y in range(2)
                        for z in range(n_seq)
                    ]
                    pieces.append(lax.ppermute(flat_qkv, ("dp", "seq"), pairs))
                    positions.append((d_at ^ dy) * n_seq + (s_at - dz) % n_seq)
        full_qkv = place(pieces, positions)
    else:
        full_qkv = lax.all_gather(flat_qkv, ("dp", "seq"), axis=0, tiled=True)
    weight_q, weight_kv = full_qkv[:, :inner], full_qkv[:, inner:]
    bias_q, bias_v = qv_bias[0:1], qv_bias[1:2]

    seg_all = [segments] + [onward(segments, t) for t in range(1, n_seq)]
    hidden_blocks = [[[chunk(hidden_in[b], i) for i in range(4)] for b in range(batch)]]
    seg_blocks = [
        [jnp.concatenate([chunk(seg_all[t][b], i) for i in range(4)], 0) for b in range(batch)]
        for t in range(n_seq)
    ]
    shard = jnp.concatenate([up_weight, down_weight, proj_weight], 1)
    shard_pieces = [shard] + [onward(shard, t) for t in range(1, n_seq)]

    def share_over_mp(piece):
        across = flip(piece, "mp", 2)
        return [piece, across, flip(piece, "mp", 1), flip(across, "mp", 1)]

    arrived = {}
    for b in range(batch):
        for t in range(1, n_seq):
            piece = hidden_blocks[0][b][0]
            if b:
                piece = after(piece, arrived[0, n_seq - 1])
            arrived[b, t] = onward(piece, t)
    for t in range(1, n_seq):
        hidden_blocks.append([share_over_mp(arrived[b, t]) for b in range(batch)])

    def limits(queries, keys):
        parts_q, parts_k = queries.reshape(-1, QB), keys.reshape(-1, KB)
        return jnp.stack([jnp.min(parts_q, 1), jnp.max(parts_q, 1), jnp.min(parts_k, 1), jnp.max(parts_k, 1)])

    bounds = [[limits(seg_blocks[0][b], seg_blocks[t][b]) for b in range(batch)] for t in range(n_seq)]
    seg_rows = [[seg_blocks[t][b].astype(F32)[None, :] for b in range(batch)] for t in range(n_seq)]

    seq_whole = place(shard_pieces, [(s_at - t) % n_seq for t in range(n_seq)])

    def over_dp(block):
        if halves:
            return block, flip(block, "dp", 1)
        return tuple(jnp.split(lax.all_gather(block, "dp", axis=0, tiled=True), 2, 0))

    near_low, near_high = over_dp(seq_whole)
    far_low, far_high = over_dp(flip(seq_whole, "mp", 2))
    low_w = [near_low, far_low, flip(near_low, "mp", 1), flip(far_low, "mp", 1)]
    high_w = [near_high, far_high, flip(near_high, "mp", 1), flip(far_high, "mp", 1)]
    up_bias_row = up_bias[None, :]
    bias_far = flip(up_bias_row, "mp", 2)
    biases = jnp.concatenate([up_bias_row, bias_far, flip(up_bias_row, "mp", 1), flip(bias_far, "mp", 1)], 0)

    queries = [None] * batch
    key_values = [[None] * batch for _ in range(n_seq)]
    state = [None] * batch
    contexts = []
    lse, out_t = [None] * batch, [None] * batch
    order = [(0, b) for b in range(batch)] + [(t, b) for b in range(batch) for t in range(1, n_seq)]
    token = None
    for t, b in order:
        first, last = t == 0, t == n_seq - 1
        segk = seg_rows[t][b]
        if token is not None:
            segk = after(segk, token)
        more = (weight_q, bias_q) if first else (queries[b], *state[b])
        outs = list(
            attend(first, last, bounds[t][b], seg_rows[0][b], segk, hidden_blocks[t][b], weight_kv, bias_v, more)
        )
        token = key_values[t][b] = outs.pop(0)
        if first:
            queries[b] = outs.pop(0)
        if last:
            contexts.append([outs[0]] + [flip(outs[i], "mp", FLIP[i]) for i in range(1, 4)])
            out_t[b], lse[b] = outs[4:]
        else:
            state[b] = outs

    vec = jnp.stack([proj_bias, first_gain, first_shift, down_bias, second_gain, second_shift])
    outs = list(
        own_rows_pass(
            halves, batch, d_at.astype(jnp.int32)[None], [c for cs in contexts for c in cs],
            own(hidden_in), own(cotangent), vec, biases, low_w, high_w,
        )
    )
    out_own, grad_first, sums, bias_sums = outs[:4]
    back, outs = outs[4 : 4 + 4 * batch], outs[4 + 4 * batch :]
    acts, pres, ctxs, transposed = outs[:4], outs[4:8], outs[8:12], outs[12:]
    back = [
        [back[b * 4]] + [flip(back[b * 4 + i], "mp", FLIP[i]) for i in range(1, 4)] for b in range(batch)
    ]
    grads = [None] * 4
    for i in (2, 3, 0, 1):
        grads[i] = weight_grads(*transposed, pres[i], acts[i], ctxs[i])

    def assemble(parts, dtype):
        whole = jnp.zeros((4, share, width), dtype)
        for i in range(4):
            whole = lax.dynamic_update_index_in_dim(whole, parts[i].astype(dtype), chunk_at ^ i, 0)
        return whole.reshape(1, local_len, width)

    def ring_sum(rows):
        parts = rows.reshape((n_seq, -1) + rows.shape[1:])
        total = None
        for t in range(1, n_seq + 1):
            part = lax.dynamic_index_in_dim(parts, (s_at - t) % n_seq, 0, keepdims=False).astype(F32)
            if total is not None:
                part = part + onward(total).astype(F32)
            total = part.astype(LOW)
        return part

    def dp_sum(mine, theirs):
        if halves:
            rows = mine.shape[0] // 2
            sent = flip(low_sum(mine[rows:], theirs[rows:]), "dp", 1).astype(F32)
            return (mine[:rows].astype(F32) + theirs[:rows].astype(F32) + sent).astype(LOW)
        return lax.psum_scatter(low_sum(mine, theirs), "dp", scatter_dimension=0, tiled=True)

    near = ring_sum(dp_sum(grads[0], flip(grads[2], "mp", 1)))
    far = ring_sum(dp_sum(grads[1], flip(grads[3], "mp", 1)))
    owned = near + flip(far.astype(LOW), "mp", 2).astype(F32)
    units = up_weight.shape[1]
    up_owned, down_owned, proj_owned = owned[:, :units], owned[:, units : 2 * units], owned[:, 2 * units :]

    out_parts = share_over_mp(out_own)
    layer_out = jnp.concatenate(
        [assemble([part[b * share : (b + 1) * share] for part in out_parts], LOW) for b in range(batch)], 0
    )

    small = jnp.concatenate([sums, bias_sums], 0)
    far_small = flip(small, "mp", 2)
    common = small[:8] + far_small[:8]
    near_bias, next_bias = small[8:9] + far_small[9:10], small[10:11] + far_small[11:12]
    small = jnp.concatenate([common, next_bias], 0)
    far_small = flip(small, "mp", 1)
    small = jnp.concatenate([common + far_small[:8], near_bias + far_small[8:]], 0)

    def over_groups(value):
        for axis, size in (("dp", n_dp), ("seq", n_seq)):
            bit = 1
            while bit < size:
                value = value + flip(value, axis, bit)
                bit *= 2
        return value

    small = over_groups(small)

    gkv = token = None
    gq = q_sum = v_sum = 0.0
    input_own = []
    input_blocks = []
    lagging = []
    for b in range(batch):
        dq = None
        extra = out_t[b]
        passing = None
        for t in list(range(1, n_seq)) + [0]:
            first, last = t == 1, t == 0
            segk = seg_rows[t][b]
            if len(lagging) >= 2:
                segk = after(segk, lagging[-2])
            outs = list(
                attend_back(
                    first, last, bounds[t][b], seg_rows[0][b], segk, hidden_blocks[t][b], back[b],
                    weight_kv, queries[b], key_values[t][b], lse[b], extra, dq, gkv, weight_q,
                )
            )
            keep, send, gkv, part = outs[:4]
            v_sum = v_sum + part[0]
            if first:
                extra = outs[4]
            if last:
                gq = gq + outs[4]
                q_sum = q_sum + outs[5][0]
            else:
                dq = outs[-1]
            theirs = flip(send, "mp", 1)
            lagging.append(theirs)
            across = flip(low_sum(keep[share:], theirs[share:]), "mp", 2)
            rows = keep[:share].astype(F32) + theirs[:share].astype(F32) + across.astype(F32)
            if passing is not None:
                rows = rows + onward(passing).astype(F32)
            passing = rows.astype(LOW)
        piece = (grad_first[b * share : (b + 1) * share] + rows).astype(LOW)
        input_blocks.append(assemble(share_over_mp(piece), F32))
    input_grad = jnp.concatenate(input_blocks, 0)
    grad_qkv = jnp.concatenate([gq, gkv], 0).astype(LOW).T
    if halves:
        rows = width // 2
        parts = grad_qkv.reshape(2, rows, 3 * inner)
        mine = lax.dynamic_index_in_dim(parts, d_at, 0, keepdims=False)
        theirs = lax.dynamic_index_in_dim(parts, 1 - d_at, 0, keepdims=False)
        grad_qkv = low_sum(mine, flip(theirs, "dp", 1))
    else:
        grad_qkv = lax.psum_scatter(grad_qkv, "dp", scatter_dimension=0, tiled=True)
    qkv_owned = ring_sum(grad_qkv).reshape(shard_rows, 3, inner)
    qv_bias_grad = over_groups(jnp.stack([q_sum, v_sum]))
    return (
        layer_out,
        input_grad,
        qkv_owned,
        qv_bias_grad,
        proj_owned,
        small[3],
        small[4],
        small[5],
        up_owned,
        small[8],
        down_owned,
        small[0],
        small[1],
        small[2],
    )


def solution(mesh):
    in_specs = (
        P("dp", "seq", None),
        P("dp", "seq"),
        P("dp", "seq", None),
        P(("dp", "seq"), None, "mp"),
        P(None, "mp"),
        P(("dp", "seq"), "mp"),
        P(),
        P(),
        P(),
        P(("dp", "seq"), "mp"),
        P("mp"),
        P(("dp", "seq"), "mp"),
        P(),
        P(),
        P(),
    )
    out_specs = (
        P("dp", "seq", None),
        P("dp", "seq", None),
        P(("dp", "seq"), None, "mp"),
        P(None, "mp"),
        P(("dp", "seq"), "mp"),
        P(),
        P(),
        P(),
        P(("dp", "seq"), "mp"),
        P("mp"),
        P(("dp", "seq"), "mp"),
        P(),
        P(),
        P(),
    )
    return jax.shard_map(shards, mesh=mesh, in_specs=in_specs, out_specs=out_specs, check_vma=False)
```

```python
import functools

import jax
import jax.numpy as jnp
from jax import lax
from jax.experimental import pallas as pl
from jax.experimental.pallas import tpu as pltpu
from jax.sharding import PartitionSpec as P

HEAD = 64
EPS = 1e-06
SCALE = HEAD**-0.5
LOG2E = 1.4426950408889634
CEXP = LOG2E * SCALE
QB = 512
KB = 512
NT = (((1,), (1,)), ((), ()))
NN = (((1,), (0,)), ((), ()))
VMEM = pl.BlockSpec(memory_space=pltpu.VMEM)
SMEM = pl.BlockSpec(memory_space=pltpu.SMEM)
LOW = jnp.bfloat16
F32 = jnp.float32
FLIP = (0, 2, 1, 3)


def dot(left, right, dims):
    return lax.dot_general(left, right, dims, preferred_element_type=F32)


def struct(shape, dtype):
    return jax.ShapeDtypeStruct(shape, dtype)


def call(body, ins, outs, scratch, mib, micros, scalars=1):
    return pl.pallas_call(
        body,
        cost_estimate=pl.CostEstimate(
            flops=int(micros * 1.1e9), bytes_accessed=1 << 20, transcendentals=0
        ),
        out_shape=tuple(outs),
        in_specs=[SMEM] * scalars + [VMEM] * (len(ins) - scalars),
        out_specs=(VMEM,) * len(outs),
        scratch_shapes=scratch,
        compiler_params=pltpu.CompilerParams(vmem_limit_bytes=mib * 2**20),
    )(*ins)


def visit(info, qrow, krow, qi, kj, work):
    qat = 2 + 4 * qrow + 2 * (qi ^ (info[0] // 2))
    kat = 2 + 4 * krow + 2 * (kj ^ (info[0] // 2))
    qlo, qhi, klo, khi = info[qat], info[qat + 1], info[kat], info[kat + 1]
    overlap = (qlo <= khi) & (klo <= qhi)
    pure = (qlo == qhi) & (klo == khi) & (qlo == klo)
    pl.when(pure)(lambda: work(False))
    pl.when(overlap & jnp.logical_not(pure))(lambda: work(True))


def fill(target, pieces):
    rows = pieces[0].shape[0]
    for i, piece in enumerate(pieces):
        target[i * rows : (i + 1) * rows, :] = piece[...]


def chunk_rows(info, i, share):
    return pl.ds(pl.multiple_of((info[0] ^ i) * share, share), share)


def load_hidden(info, b, target, pieces):
    if len(pieces) > 1:
        fill(target, pieces)
        return
    share = target.shape[0] // 4
    for i in range(4):
        target[i * share : (i + 1) * share, :] = pieces[0][b, chunk_rows(info, i, share), :]


def load_segments(info, qrow, krow, segs, segq, segc):
    share = segq.shape[1] // 4
    for i in range(4):
        cols = chunk_rows(info, i, share)
        own = slice(i * share, (i + 1) * share)
        segq[:, own] = jnp.broadcast_to(segs[qrow : qrow + 1, cols], (8, share))
        segc[own, :] = jnp.broadcast_to(segs[krow : krow + 1, cols], (128, share)).astype(F32).T.astype(jnp.int32)


def fwd_body(first, last, gather, b, qrow, krow, count, info, segs, *refs):
    refs = list(refs)
    pieces = [refs.pop(0) for _ in range(count)]
    if gather:
        shards = [refs.pop(0) for _ in range(gather)]
        vbias = refs.pop(0)
    else:
        wkv, vbias = refs.pop(0), refs.pop(0)
    if first:
        if not gather:
            wq = refs.pop(0)
        qbias = refs.pop(0)
        before = None
    else:
        q = refs.pop(0)
        before = [refs.pop(0) for _ in range(3)]
    if gather:
        wq, wkv = refs.pop(0), refs.pop(0)
    kv = refs.pop(0)
    if first:
        q = refs.pop(0)
    if last:
        contexts = [refs.pop(0) for _ in range(4)]
        out_t, lse = refs.pop(0), refs.pop(0)
    top, total, acc = refs.pop(0), refs.pop(0), refs.pop(0)
    hidden, vt, segq, segc = refs
    inner = q.shape[1]
    load_hidden(info, b, hidden, pieces)
    load_segments(info, qrow, krow, segs, segq, segc)
    for j in range(gather):
        height = shards[j].shape[0]
        at = 0
        if gather > 1:
            n_seq = gather // 2
            back = info[info.shape[0] - 1] - j % n_seq
            at = (info[1] ^ (j // n_seq)) * n_seq + jnp.where(back < 0, back + n_seq, back)
        rows = pl.ds(pl.multiple_of(at * height, height), height)
        wq[rows, :] = shards[j][:, :inner]
        wkv[rows, :] = shards[j][:, inner : 3 * inner]
    value = dot(hidden[...], wkv[...], NN)
    kv[:, :inner] = value[:, :inner].astype(LOW)
    value = value[:, inner:] + vbias[...]
    kv[:, inner:] = value.astype(LOW)
    vt[...] = value.T.astype(LOW)
    if first:
        q[...] = (dot(hidden[...], wq[...], NN) + qbias[...]).astype(LOW)
        top[...] = jnp.full(top.shape, -1e30, F32)
        total[...] = jnp.zeros(total.shape, F32)
        acc[...] = jnp.zeros(acc.shape, F32)
    else:
        top[...], total[...], acc[...] = (ref[...] for ref in before)

    def qstep(qi, _):
        qs = pl.ds(pl.multiple_of(qi * QB, QB), QB)

        def kstep(kj, _):
            ks = pl.ds(pl.multiple_of(kj * KB, KB), KB)

            def work(masked):
                if masked:
                    bad = segc[ks, 0:1] != segq[0:1, qs]
                for h in range(inner // HEAD):
                    c = slice(h * HEAD, (h + 1) * HEAD)
                    s = dot(kv[ks, c], q[qs, c], NT) * CEXP
                    if masked:
                        s = jnp.where(bad, -1e30, s)
                    old = top[h : h + 1, qs]
                    new = jnp.maximum(old, jnp.max(s, 0, keepdims=True))
                    p = jnp.exp2(s - new)
                    shrink = jnp.exp2(old - new)
                    top[h : h + 1, qs] = new
                    total[h : h + 1, qs] = total[h : h + 1, qs] * shrink + jnp.sum(p, 0, keepdims=True)
                    acc[c, qs] = acc[c, qs] * shrink + dot(vt[c, ks], p.astype(LOW), NN)

            visit(info, qrow, krow, qi, kj, work)
            return 0

        lax.fori_loop(0, kv.shape[0] // KB, kstep, 0)
        return 0

    lax.fori_loop(0, q.shape[0] // QB, qstep, 0)
    if last:
        for h in range(inner // HEAD):
            c = slice(h * HEAD, (h + 1) * HEAD)
            out_t[c, :] = acc[c, :] / total[h : h + 1, :]
            lse[h : h + 1, :] = top[h : h + 1, :] + jnp.log(total[h : h + 1, :]) * LOG2E
        natural = out_t[...].T.astype(LOW)
        rows = contexts[0].shape[0]
        for i in range(4):
            contexts[i][...] = natural[i * rows : (i + 1) * rows, :]


def attend(first, last, gather, b, t, batch, inner, info, segs, pieces, more):
    rows, width = pieces[-1].shape[-2:]
    rows = rows if len(pieces) == 1 else 4 * rows
    stats = [((8, rows), F32), ((8, rows), F32), ((inner, rows), F32)]
    outs = []
    if gather:
        outs += [struct((width, inner), LOW), struct((width, 2 * inner), LOW)]
    outs.append(struct((rows, 2 * inner), LOW))
    if first:
        outs.append(struct((rows, inner), LOW))
    if last:
        outs += [struct((rows // 4, inner), LOW)] * 4 + [struct((inner, rows), F32), struct((8, rows), F32)]
    else:
        outs += [struct(*item) for item in stats]
    scratch = [pltpu.VMEM(*item) for item in stats] if last else []
    scratch += [pltpu.VMEM((rows, width), LOW), pltpu.VMEM((inner, rows), LOW)]
    scratch += [pltpu.VMEM((8, rows), jnp.int32), pltpu.VMEM((rows, 128), jnp.int32)]
    body = functools.partial(fwd_body, first, last, gather, b, b, t * batch + b, len(pieces))
    return call(body, [info, segs, *pieces, *more], outs, scratch, 24, 9)


def bwd_body(first, last, add, again, b, qrow, krow, count, info, segs, *refs):
    refs = list(refs)
    pieces = [refs.pop(0) for _ in range(count)]
    back = [refs.pop(0) for _ in range(4)]
    wkv, q, kv, lse, extra = (refs.pop(0) for _ in range(5))
    if not first:
        dq_before = refs.pop(0)
    if add:
        gkv_before, vsum_before = refs.pop(0), refs.pop(0)
    if last:
        wq = refs.pop(0)
    if again:
        gq_before, qsum_before = refs.pop(0), refs.pop(0)
    keep, send, gkv, vsum = (refs.pop(0) for _ in range(4))
    if first:
        delta = refs.pop(0)
    else:
        delta = extra
    if last:
        gq, qsum = refs.pop(0), refs.pop(0)
    dq = refs.pop(0)
    hidden, do, kt, segq, segc, dk, dv, dkv = refs
    inner = q.shape[1]
    load_hidden(info, b, hidden, pieces)
    fill(do, back)
    load_segments(info, qrow, krow, segs, segq, segc)
    kt[...] = kv[:, :inner].astype(F32).T.astype(LOW)
    if first:
        product = do[...].astype(F32).T * extra[...]
        delta[...] = jnp.zeros(delta.shape, F32)
        for h in range(inner // HEAD):
            delta[h : h + 1, :] = jnp.sum(product[h * HEAD : (h + 1) * HEAD, :], 0, keepdims=True)
        dq[...] = jnp.zeros(dq.shape, F32)
    else:
        dq[...] = dq_before[...]
    dk[...] = jnp.zeros(dk.shape, F32)
    dv[...] = jnp.zeros(dv.shape, F32)

    def kstep(kj, _):
        ks = pl.ds(pl.multiple_of(kj * KB, KB), KB)

        def qstep(qi, _):
            qs = pl.ds(pl.multiple_of(qi * QB, QB), QB)

            def work(masked):
                if masked:
                    bad = segc[ks, 0:1] != segq[0:1, qs]
                for h in range(inner // HEAD):
                    c = slice(h * HEAD, (h + 1) * HEAD)
                    cv = slice(inner + h * HEAD, inner + (h + 1) * HEAD)
                    qh = q[qs, c]
                    dh = do[qs, c]
                    s = dot(kv[ks, c], qh, NT) * CEXP - lse[h : h + 1, qs]
                    if masked:
                        s = jnp.where(bad, -1e30, s)
                    p = jnp.exp2(s)
                    dp = dot(kv[ks, cv], dh, NT)
                    ds = (p * (dp - delta[h : h + 1, qs])).astype(LOW)
                    dv[ks, c] += dot(p.astype(LOW), dh, NN)
                    dk[ks, c] += dot(ds, qh, NN)
                    dq[c, qs] += dot(kt[c, ks], ds, NN)

            visit(info, qrow, krow, qi, kj, work)
            return 0

        lax.fori_loop(0, q.shape[0] // QB, qstep, 0)
        return 0

    lax.fori_loop(0, kv.shape[0] // KB, kstep, 0)
    dkv[:, :inner] = (dk[...] * SCALE).astype(LOW)
    dkv[:, inner:] = dv[...].astype(LOW)
    total = jnp.broadcast_to(jnp.sum(dv[...], 0, keepdims=True), vsum.shape)
    vsum[...] = vsum_before[...] + total if add else total
    half = keep.shape[0]
    if last:
        dq_low = (dq[...] * SCALE).T
        total = jnp.broadcast_to(jnp.sum(dq_low, 0, keepdims=True), qsum.shape)
        qsum[...] = qsum_before[...] + total if again else total
        dq_low = dq_low.astype(LOW)
        value = dot((dq[...] * SCALE).astype(LOW), hidden[...], NN)
        gq[...] = gq_before[...] + value if again else value
    for part, out in ((slice(0, half), keep), (slice(half, 2 * half), send)):
        value = dot(dkv[part, :], wkv[...], NT)
        if last:
            value = value + dot(dq_low[part, :], wq[...], NT)
        out[...] = value.astype(LOW)
    parts = [(dk[...] * SCALE).T.astype(LOW), dv[...].T.astype(LOW)]
    for i in range(2):
        rows = slice(i * inner, (i + 1) * inner)
        value = dot(parts[i], hidden[...], NN)
        gkv[rows, :] = gkv_before[rows, :] + value if add else value


def attend_back(first, last, b, t, batch, info, segs, pieces, back, wkv, q, kv, lse, extra, dq, sums, wq, more):
    rows, inner = q.shape
    width = wkv.shape[0]
    outs = [struct((rows // 2, width), LOW)] * 2 + [struct((2 * inner, width), F32), struct((8, inner), F32)]
    if first:
        outs.append(struct((8, rows), F32))
    if last:
        outs += [struct((inner, width), F32), struct((8, inner), F32)]
    scratch = []
    if last:
        scratch.append(pltpu.VMEM((inner, rows), F32))
    else:
        outs.append(struct((inner, rows), F32))
    scratch += [
        pltpu.VMEM((rows, width), LOW),
        pltpu.VMEM((rows, inner), LOW),
        pltpu.VMEM((inner, rows), LOW),
        pltpu.VMEM((8, rows), jnp.int32),
        pltpu.VMEM((rows, 128), jnp.int32),
        pltpu.VMEM((rows, inner), F32),
        pltpu.VMEM((rows, inner), F32),
        pltpu.VMEM((rows, 2 * inner), LOW),
    ]
    ins = [info, segs, *pieces, *back, wkv, q, kv, lse, extra]
    ins += [] if first else [dq]
    ins += [*sums]
    ins += [wq, *more] if last else []
    body = functools.partial(
        bwd_body, first, last, len(sums) > 0, last and len(more) > 0, b, b, t * batch + b, len(pieces)
    )
    return call(body, ins, outs, scratch, 28, 12)


def assemble_body(info, *refs):
    parts, out = refs[:4], refs[-1]
    share = parts[0].shape[0]
    for i in range(4):
        out[0, chunk_rows(info, i, share), :] = parts[i][...].astype(out.dtype)


def assemble(info, parts, batch, share, dtype, at, whole):
    count, width = parts[0].shape[0] // share, parts[0].shape[1]
    specs = [SMEM] + [pl.BlockSpec((share, width), lambda i: (i, 0))] * 4
    ins = [info, *parts]
    if whole is not None:
        ins.append(whole)
        specs.append(pl.BlockSpec(memory_space=pl.ANY))
    return pl.pallas_call(
        assemble_body,
        grid=(count,),
        cost_estimate=pl.CostEstimate(flops=int(2e9), bytes_accessed=1 << 20, transcendentals=0),
        out_shape=struct((batch, 4 * share, width), dtype),
        in_specs=specs,
        out_specs=pl.BlockSpec((1, 4 * share, width), lambda i: (i + at, 0, 0)),
        input_output_aliases={} if whole is None else {5: 0},
        compiler_params=pltpu.CompilerParams(vmem_limit_bytes=16 * 2**20),
    )(*ins)


def finish_body(info, gq, gkv, *refs):
    outs, whole = refs[:-1], refs[-1]
    inner = gq.shape[0]
    whole[...] = jnp.zeros(whole.shape, F32)
    whole[:inner, :] = gq[...]
    whole[inner : 3 * inner, :] = gkv[...]
    rows = outs[0].shape[0]
    if len(outs) == 1:
        outs[0][...] = whole[...].T.astype(LOW)
        return
    first, second = whole[:, :rows].T.astype(LOW), whole[:, rows:].T.astype(LOW)
    low = info[1] == 0
    outs[0][...] = jnp.where(low, first, second)
    outs[1][...] = jnp.where(low, second, first)


def finish_qkv(halves, info, gq, gkv):
    inner, width = gq.shape
    columns = -(-3 * inner // 128) * 128
    rows = width // 2 if halves else width
    outs = [struct((rows, columns), LOW)] * (2 if halves else 1)
    return call(finish_body, [info, gq, gkv], outs, [pltpu.VMEM((columns, width), F32)], 20, 2)


def rows_body(halves, batch, info, *refs):
    refs = list(refs)
    take = lambda count: [refs.pop(0) for _ in range(count)]
    ctx_in = take(4 * batch)
    hidden, cot, vec, bias = take(4)
    low_w, high_w = take(4), take(4)
    out_low, grad_first, sums, bias_sums = take(4)
    back = take(4 * batch)
    acts, pres, ctxs = take(4), take(4), take(4)
    nl_t, dl_t, al_t = take(3)
    slopes = take(4)
    width = hidden.shape[1]
    half = width // 2
    units, inner = bias.shape[1], ctxs[0].shape[1]
    up, down, proj = slice(0, units), slice(units, 2 * units), slice(2 * units, 2 * units + inner)

    def swapped(value):
        if not halves:
            return value
        turned = jnp.concatenate([value[:, half:], value[:, :half]], 1)
        return jnp.where(info[1] == 1, turned, value)

    def into(value, r, cols):
        return dot(value[:, :half], low_w[r][:, cols], NN) + dot(value[:, half:], high_w[r][:, cols], NN)

    def out_of(value, r, cols):
        return jnp.concatenate([dot(value, low_w[r][:, cols], NT), dot(value, high_w[r][:, cols], NT)], 1)

    def norm(value):
        center = value - jnp.mean(value, -1, keepdims=True)
        inverse = lax.rsqrt(jnp.mean(center * center, -1, keepdims=True) + EPS)
        return center * inverse, inverse

    def norm_back(grad, unit, inverse):
        shared = jnp.mean(grad, -1, keepdims=True)
        return inverse * (grad - shared - unit * jnp.mean(grad * unit, -1, keepdims=True))

    attn = None
    for r in range(4):
        fill(ctxs[r], [ctx_in[b * 4 + r] for b in range(batch)])
        part = out_of(ctxs[r][...], r, proj)
        attn = part if attn is None else attn + part
    unit_one, inverse_one = norm(hidden[...].astype(F32) + swapped(attn) + vec[0:1, :])
    normed = unit_one * vec[1:2, :] + vec[2:3, :]
    normed_sw = swapped(normed)
    nl_t[...] = normed_sw.T.astype(LOW)
    normed_low = normed_sw.astype(LOW)
    total = None
    for r in range(4):
        pre = into(normed_low, r, up) + bias[r : r + 1, :]
        gate = 0.5 + 0.5 * lax.erf(pre * 0.7071067811865476)
        acts[r][...] = (pre * gate).astype(LOW)
        slopes[r][...] = gate + pre * (0.3989422804014327 * jnp.exp(-0.5 * pre * pre))
        part = out_of(acts[r][...], r, down)
        total = part if total is None else total + part
    unit_two, inverse_two = norm(normed + swapped(total) + vec[3:4, :])
    out_low[...] = (unit_two * vec[4:5, :] + vec[5:6, :]).astype(LOW)
    cotangent = cot[...].astype(F32)
    grad_second = norm_back(cotangent * vec[4:5, :], unit_two, inverse_two)
    sums[...] = jnp.zeros(sums.shape, F32)
    sums[0:1, :] = jnp.sum(grad_second, 0, keepdims=True)
    sums[1:2, :] = jnp.sum(cotangent * unit_two, 0, keepdims=True)
    sums[2:3, :] = jnp.sum(cotangent, 0, keepdims=True)
    second_sw = swapped(grad_second)
    dl_t[...] = second_sw.T.astype(LOW)
    down_low = second_sw.astype(LOW)
    total = None
    for r in range(4):
        pre_low = (into(down_low, r, down) * slopes[r][...]).astype(LOW)
        pres[r][...] = pre_low
        bias_sums[r : r + 1, :] = jnp.sum(pre_low.astype(F32), 0, keepdims=True)
        part = out_of(pre_low, r, up)
        total = part if total is None else total + part
    grad_normed = grad_second + swapped(total)
    first = norm_back(grad_normed * vec[1:2, :], unit_one, inverse_one)
    grad_first[...] = first
    sums[3:4, :] = jnp.sum(first, 0, keepdims=True)
    sums[4:5, :] = jnp.sum(grad_normed * unit_one, 0, keepdims=True)
    sums[5:6, :] = jnp.sum(grad_normed, 0, keepdims=True)
    first_sw = swapped(first)
    al_t[...] = first_sw.T.astype(LOW)
    attn_low = first_sw.astype(LOW)
    share = back[0].shape[0]
    for r in range(4):
        value = into(attn_low, r, proj).astype(LOW)
        for b in range(batch):
            back[b * 4 + r][...] = value[b * share : (b + 1) * share, :]


def own_rows_pass(halves, batch, flag, ctx, hidden, cot, vec, bias, low_w, high_w):
    rows, width = hidden.shape
    share, inner = ctx[0].shape
    units = bias.shape[1]
    outs = [struct((rows, width), LOW), struct((rows, width), F32), struct((8, width), F32), struct((4, units), F32)]
    outs += [struct((share, inner), LOW)] * (4 * batch)
    outs += [struct((rows, units), LOW)] * 8 + [struct((rows, inner), LOW)] * 4
    outs += [struct((width, rows), LOW)] * 3
    ins = [flag, *ctx, hidden, cot, vec, bias, *low_w, *high_w]
    scratch = [pltpu.VMEM((rows, units), F32)] * 4
    return call(functools.partial(rows_body, halves, batch), ins, outs, scratch, 40, 26)


def grads_body(nl_t, dl_t, al_t, pre, act, ctx, out):
    units = act.shape[1]
    out[:, :units] = dot(nl_t[...], pre[...], NN).astype(LOW)
    out[:, units : 2 * units] = dot(dl_t[...], act[...], NN).astype(LOW)
    inner = ctx.shape[1]
    out[:, 2 * units : 2 * units + inner] = dot(al_t[...], ctx[...], NN).astype(LOW)
    out[:, 2 * units + inner :] = jnp.zeros((out.shape[0], out.shape[1] - 2 * units - inner), LOW)


def weight_grads(nl_t, dl_t, al_t, pre, act, ctx):
    shape = (nl_t.shape[0], -(-(2 * act.shape[1] + ctx.shape[1]) // 128) * 128)
    return call(grads_body, [nl_t, dl_t, al_t, pre, act, ctx], [struct(shape, LOW)], [], 20, 2, 0)[0]


def flip(value, axis, bit):
    size = lax.axis_size(axis)
    return lax.ppermute(value, axis, [(i, i ^ bit) for i in range(size)])


def onward(value, step=1):
    size = lax.axis_size("seq")
    return lax.ppermute(value, "seq", [(i, (i + step) % size) for i in range(size)])


def after(value, *others):
    return lax.optimization_barrier((value,) + others)[0]


def low_sum(left, right):
    return (left.astype(F32) + right.astype(F32)).astype(LOW)


def shards(
    hidden_in,
    segments,
    cotangent,
    qkv_weight,
    qv_bias,
    proj_weight,
    proj_bias,
    first_gain,
    first_shift,
    up_weight,
    up_bias,
    down_weight,
    down_bias,
    second_gain,
    second_shift,
):
    batch, local_len, width = hidden_in.shape
    inner = qkv_weight.shape[2]
    n_dp, n_seq, n_mp = lax.axis_size("dp"), lax.axis_size("seq"), lax.axis_size("mp")
    assert n_mp == 4
    d_at, s_at, m_at = lax.axis_index("dp"), lax.axis_index("seq"), lax.axis_index("mp")
    chunk_at = (m_at % 2) * 2 + m_at // 2
    share = local_len // n_mp
    shard_rows = qkv_weight.shape[0]
    halves = n_dp == 2

    def place(pieces, positions):
        whole = jnp.zeros((len(pieces),) + pieces[0].shape, pieces[0].dtype)
        for piece, position in zip(pieces, positions):
            whole = lax.dynamic_update_index_in_dim(whole, piece, position, 0)
        return whole.reshape((-1,) + pieces[0].shape[1:])

    def chunk(rows, i):
        parts = rows.reshape((4, share) + rows.shape[1:])
        return lax.dynamic_index_in_dim(parts, chunk_at ^ i, 0, keepdims=False)

    def own(rows):
        return jnp.concatenate([chunk(rows[b], 0) for b in range(batch)], 0)

    spare = jnp.zeros((shard_rows, -3 * inner % 128), LOW)
    flat_qkv = jnp.concatenate([qkv_weight.reshape(shard_rows, 3 * inner), spare], 1)
    if halves:
        qkv_shards = [flat_qkv]
        for dy in range(2):
            for dz in range(n_seq):
                if dy or dz:
                    pairs = [
                        (y * n_seq + z, (y ^ dy) * n_seq + (z + dz) % n_seq)
                        for y in range(2)
                        for z in range(n_seq)
                    ]
                    qkv_shards.append(lax.ppermute(flat_qkv, ("dp", "seq"), pairs))
    else:
        qkv_shards = [lax.all_gather(flat_qkv, ("dp", "seq"), axis=0, tiled=True)]
    bias_q, bias_v = qv_bias[0:1], qv_bias[1:2]

    seg_all = [segments] + [onward(segments, t) for t in range(1, n_seq)]
    segs = jnp.concatenate(seg_all, 0)
    edges = segs.reshape(-1, 2, local_len // 2)[:, :, :: local_len // 2 - 1].reshape(-1)
    info = jnp.concatenate([jnp.stack([chunk_at, d_at]), edges, s_at[None]]).astype(jnp.int32)
    hidden_blocks = [[[hidden_in] for b in range(batch)]]
    own_chunks = [chunk(hidden_in[b], 0) for b in range(batch)]
    spare = jnp.zeros((shard_rows, -(2 * up_weight.shape[1] + inner) % 128), LOW)
    shard = jnp.concatenate([up_weight, down_weight, proj_weight, spare], 1)
    shard_pieces = [shard] + [onward(shard, t) for t in range(1, n_seq)]

    def share_over_mp(piece):
        across = flip(piece, "mp", 2)
        return [piece, across, flip(piece, "mp", 1), flip(across, "mp", 1)]

    arrived = {}
    for b in range(batch):
        for t in range(1, n_seq):
            piece = own_chunks[b]
            if b:
                piece = after(piece, arrived[0, n_seq - 1])
            arrived[b, t] = onward(piece, t)
    for t in range(1, n_seq):
        hidden_blocks.append([share_over_mp(arrived[b, t]) for b in range(batch)])

    seq_whole = place(shard_pieces, [(s_at - t) % n_seq for t in range(n_seq)])

    def over_dp(block):
        if halves:
            return block, flip(block, "dp", 1)
        return tuple(jnp.split(lax.all_gather(block, "dp", axis=0, tiled=True), 2, 0))

    near_low, near_high = over_dp(seq_whole)
    far_low, far_high = over_dp(flip(seq_whole, "mp", 2))
    low_w = [near_low, far_low, flip(near_low, "mp", 1), flip(far_low, "mp", 1)]
    high_w = [near_high, far_high, flip(near_high, "mp", 1), flip(far_high, "mp", 1)]
    up_bias_row = up_bias[None, :]
    bias_far = flip(up_bias_row, "mp", 2)
    biases = jnp.concatenate([up_bias_row, bias_far, flip(up_bias_row, "mp", 1), flip(bias_far, "mp", 1)], 0)

    queries = [None] * batch
    key_values = [[None] * batch for _ in range(n_seq)]
    state = [None] * batch
    contexts = []
    lse, out_t = [None] * batch, [None] * batch
    order = [(0, b) for b in range(batch)] + [(t, b) for b in range(batch) for t in range(1, n_seq)]
    token = weight_q = weight_kv = None
    waits = {2: [seq_whole], 5: [far_low, near_high]}
    for step, (t, b) in enumerate(order):
        first, last = t == 0, t == n_seq - 1
        gather = len(qkv_shards) if step == 0 else 0
        more = (*qkv_shards, bias_v) if gather else (weight_kv, bias_v)
        if first:
            more += (bias_q,) if gather else (weight_q, bias_q)
        else:
            more += (queries[b], *state[b])
        held = info if token is None else after(info, token, *waits.get(step, []))
        outs = list(attend(first, last, gather, b, t, batch, inner, held, segs, hidden_blocks[t][b], more))
        if gather:
            weight_q, weight_kv = outs.pop(0), outs.pop(0)
        token = key_values[t][b] = outs.pop(0)
        if first:
            queries[b] = outs.pop(0)
        if last:
            contexts.append([outs[0]] + [flip(outs[i], "mp", FLIP[i]) for i in range(1, 4)])
            out_t[b], lse[b] = outs[4:]
        else:
            state[b] = outs

    vec = jnp.stack([proj_bias, first_gain, first_shift, down_bias, second_gain, second_shift])
    outs = list(
        own_rows_pass(
            halves, batch, info, [c for cs in contexts for c in cs],
            jnp.concatenate(own_chunks, 0), own(cotangent), vec, biases, low_w, high_w,
        )
    )
    out_own, grad_first, sums, bias_sums = outs[:4]
    back, outs = outs[4 : 4 + 4 * batch], outs[4 + 4 * batch :]
    acts, pres, ctxs, transposed = outs[:4], outs[4:8], outs[8:12], outs[12:]
    back = [
        [back[b * 4]] + [flip(back[b * 4 + i], "mp", FLIP[i]) for i in range(1, 4)] for b in range(batch)
    ]
    grads = [None] * 4
    for i in (2, 3, 0, 1):
        grads[i] = weight_grads(*transposed, pres[i], acts[i], ctxs[i])

    def ring_sum(rows):
        parts = rows.reshape((n_seq, -1) + rows.shape[1:])
        total = None
        hops = []
        for t in range(1, n_seq + 1):
            part = lax.dynamic_index_in_dim(parts, (s_at - t) % n_seq, 0, keepdims=False).astype(F32)
            if total is not None:
                part = part + onward(total).astype(F32)
            total = part.astype(LOW)
            hops.append(total)
        return hops[:-1] + [part]

    def dp_sum(mine, theirs):
        if halves:
            rows = mine.shape[0] // 2
            sent = flip(low_sum(mine[rows:], theirs[rows:]), "dp", 1).astype(F32)
            return (mine[:rows].astype(F32) + theirs[:rows].astype(F32) + sent).astype(LOW)
        return lax.psum_scatter(low_sum(mine, theirs), "dp", scatter_dimension=0, tiled=True)

    near_in, far_in = flip(grads[2], "mp", 1), flip(grads[3], "mp", 1)
    near_half, far_half = dp_sum(grads[0], near_in), dp_sum(grads[1], far_in)
    near_hops, far_hops = ring_sum(near_half), ring_sum(far_half)
    owned = near_hops[-1] + flip(far_hops[-1].astype(LOW), "mp", 2).astype(F32)
    units = up_weight.shape[1]
    up_owned, down_owned = owned[:, :units], owned[:, units : 2 * units]
    proj_owned = owned[:, 2 * units : 2 * units + inner]

    layer_out = assemble(info, share_over_mp(out_own), batch, share, LOW, 0, None)

    small = jnp.concatenate([sums, bias_sums], 0)
    far_small = flip(small, "mp", 2)
    common = small[:8] + far_small[:8]
    near_bias, next_bias = small[8:9] + far_small[9:10], small[10:11] + far_small[11:12]
    small = jnp.concatenate([common, next_bias], 0)
    far_small = flip(small, "mp", 1)
    small = jnp.concatenate([common + far_small[:8], near_bias + far_small[8:]], 0)

    def over_groups(value):
        for axis, size in (("dp", n_dp), ("seq", n_seq)):
            bit = 1
            while bit < size:
                value = value + flip(value, axis, bit)
                bit *= 2
        return value

    small = over_groups(small)

    sums, more = (), ()
    input_grad = None
    theirs_of, passing_of = [], []
    waits = {
        1: [near_in, far_in],
        2: [layer_out],
        3: [small],
        4: [near_half],
        5: [far_half, near_hops[0]],
        6: [near_hops[1], far_hops[0]],
        7: [near_hops[2], far_hops[1]],
    }
    for b in range(batch):
        dq = None
        extra = out_t[b]
        passing = None
        for t in list(range(1, n_seq)) + [0]:
            first, last = t == 1, t == 0
            step = len(theirs_of)
            waiting = waits.get(step, [])
            waiting = waiting + theirs_of[max(step - 2, 0) : max(step - 1, 0)]
            waiting = waiting + passing_of[max(step - 4, 0) : max(step - 3, 0)]
            held = after(info, *waiting) if waiting else info
            outs = list(
                attend_back(
                    first, last, b, t, batch, held, segs, hidden_blocks[t][b], back[b], weight_kv,
                    queries[b], key_values[t][b], lse[b], extra, dq, sums, weight_q, more,
                )
            )
            keep, send = outs[:2]
            sums = outs[2:4]
            if first:
                extra = outs[4]
            if last:
                more = outs[4:6]
            else:
                dq = outs[-1]
            theirs = flip(send, "mp", 1)
            theirs_of.append(theirs)
            across = flip(low_sum(keep[share:], theirs[share:]), "mp", 2)
            rows = keep[:share].astype(F32) + theirs[:share].astype(F32) + across.astype(F32)
            if passing is not None:
                rows = rows + onward(passing).astype(F32)
            passing = rows.astype(LOW)
            passing_of.append(passing)
        piece = (grad_first[b * share : (b + 1) * share] + rows).astype(LOW)
        input_grad = assemble(info, share_over_mp(piece), batch, share, F32, b, input_grad)
    gq, q_sum = more
    gkv, v_sum = sums
    finished = finish_qkv(halves, info, gq, gkv)
    if halves:
        grad_qkv = low_sum(finished[0], flip(finished[1], "dp", 1))
    else:
        grad_qkv = lax.psum_scatter(finished[0], "dp", scatter_dimension=0, tiled=True)
    qkv_owned = ring_sum(grad_qkv)[-1][:, : 3 * inner].reshape(shard_rows, 3, inner)
    qv_bias_grad = over_groups(jnp.concatenate([q_sum[:1], v_sum[:1]], 0))
    return (
        layer_out,
        input_grad,
        qkv_owned,
        qv_bias_grad,
        proj_owned,
        small[3],
        small[4],
        small[5],
        up_owned,
        small[8],
        down_owned,
        small[0],
        small[1],
        small[2],
    )


def solution(mesh):
    in_specs = (
        P("dp", "seq", None),
        P("dp", "seq"),
        P("dp", "seq", None),
        P(("dp", "seq"), None, "mp"),
        P(None, "mp"),
        P(("dp", "seq"), "mp"),
        P(),
        P(),
        P(),
        P(("dp", "seq"), "mp"),
        P("mp"),
        P(("dp", "seq"), "mp"),
        P(),
        P(),
        P(),
    )
    out_specs = (
        P("dp", "seq", None),
        P("dp", "seq", None),
        P(("dp", "seq"), None, "mp"),
        P(None, "mp"),
        P(("dp", "seq"), "mp"),
        P(),
        P(),
        P(),
        P(("dp", "seq"), "mp"),
        P("mp"),
        P(("dp", "seq"), "mp"),
        P(),
        P(),
        P(),
    )
    return jax.shard_map(shards, mesh=mesh, in_specs=in_specs, out_specs=out_specs, check_vma=False)
```

```python
import functools

import jax
import jax.numpy as jnp
from jax import lax
from jax.experimental import pallas as pl
from jax.experimental.pallas import tpu as pltpu
from jax.sharding import PartitionSpec as P

HEAD = 64
EPS = 1e-06
SCALE = HEAD**-0.5
LOG2E = 1.4426950408889634
CEXP = LOG2E * SCALE
QB = 512
KB = 512
NT = (((1,), (1,)), ((), ()))
NN = (((1,), (0,)), ((), ()))
VMEM = pl.BlockSpec(memory_space=pltpu.VMEM)
SMEM = pl.BlockSpec(memory_space=pltpu.SMEM)
LOW = jnp.bfloat16
F32 = jnp.float32
FLIP = (0, 2, 1, 3)


def dot(left, right, dims):
    return lax.dot_general(left, right, dims, preferred_element_type=F32)


def struct(shape, dtype):
    return jax.ShapeDtypeStruct(shape, dtype)


def call(body, ins, outs, scratch, mib, micros, scalars=1):
    return pl.pallas_call(
        body,
        cost_estimate=pl.CostEstimate(
            flops=int(micros * 1.1e9), bytes_accessed=1 << 20, transcendentals=0
        ),
        out_shape=tuple(outs),
        in_specs=[SMEM] * scalars + [VMEM] * (len(ins) - scalars),
        out_specs=(VMEM,) * len(outs),
        scratch_shapes=scratch,
        compiler_params=pltpu.CompilerParams(vmem_limit_bytes=mib * 2**20),
    )(*ins)


def visit(info, qrow, krow, qi, kj, work):
    qat = 2 + 4 * qrow + 2 * (qi ^ (info[0] // 2))
    kat = 2 + 4 * krow + 2 * (kj ^ (info[0] // 2))
    qlo, qhi, klo, khi = info[qat], info[qat + 1], info[kat], info[kat + 1]
    overlap = (qlo <= khi) & (klo <= qhi)
    pure = (qlo == qhi) & (klo == khi) & (qlo == klo)
    pl.when(pure)(lambda: work(False))
    pl.when(overlap & jnp.logical_not(pure))(lambda: work(True))


def fill(target, pieces):
    rows = pieces[0].shape[0]
    for i, piece in enumerate(pieces):
        target[i * rows : (i + 1) * rows, :] = piece[...]


def chunk_rows(info, i, share):
    return pl.ds(pl.multiple_of((info[0] ^ i) * share, share), share)


def load_hidden(info, b, target, pieces):
    share = target.shape[0] // 4
    if len(pieces) > 1:
        for i in range(4):
            target[i * share : (i + 1) * share, :] = pieces[i][b * share : (b + 1) * share, :]
        return
    for i in range(4):
        target[i * share : (i + 1) * share, :] = pieces[0][b, chunk_rows(info, i, share), :]


def load_segments(info, qrow, krow, segs, segq, segc):
    share = segq.shape[1] // 4
    for i in range(4):
        cols = chunk_rows(info, i, share)
        own = slice(i * share, (i + 1) * share)
        segq[:, own] = jnp.broadcast_to(segs[qrow : qrow + 1, cols], (8, share))
        segc[own, :] = jnp.broadcast_to(segs[krow : krow + 1, cols], (128, share)).astype(F32).T.astype(jnp.int32)


def fwd_body(first, last, gather, b, qrow, krow, count, info, segs, *refs):
    refs = list(refs)
    pieces = [refs.pop(0) for _ in range(count)]
    if gather:
        shards = [refs.pop(0) for _ in range(gather)]
        vbias = refs.pop(0)
    else:
        wkv, vbias = refs.pop(0), refs.pop(0)
    if first:
        if not gather:
            wq = refs.pop(0)
        qbias = refs.pop(0)
        before = None
    else:
        q = refs.pop(0)
        before = [refs.pop(0) for _ in range(3)]
    if gather:
        wq, wkv = refs.pop(0), refs.pop(0)
    kv = refs.pop(0)
    if first:
        q = refs.pop(0)
    if last:
        contexts = [refs.pop(0) for _ in range(4)]
        out_t, lse = refs.pop(0), refs.pop(0)
    top, total, acc = refs.pop(0), refs.pop(0), refs.pop(0)
    hidden, vt, segq, segc = refs
    inner = q.shape[1]
    load_hidden(info, b, hidden, pieces)
    load_segments(info, qrow, krow, segs, segq, segc)
    for j in range(gather):
        parts = 1 if gather == 1 else 2
        height = shards[j].shape[0] // parts
        for y in range(parts):
            at = 0
            if parts == 2:
                back = info[info.shape[0] - 1] - j
                at = (info[1] ^ y) * gather + jnp.where(back < 0, back + gather, back)
            rows = pl.ds(pl.multiple_of(at * height, height), height)
            source = slice(y * height, (y + 1) * height)
            wq[rows, :] = shards[j][source, :inner]
            wkv[rows, :] = shards[j][source, inner : 3 * inner]
    value = dot(hidden[...], wkv[...], NN)
    kv[:, :inner] = value[:, :inner].astype(LOW)
    value = value[:, inner:] + vbias[...]
    kv[:, inner:] = value.astype(LOW)
    vt[...] = value.T.astype(LOW)
    if first:
        q[...] = (dot(hidden[...], wq[...], NN) + qbias[...]).astype(LOW)
        top[...] = jnp.full(top.shape, -1e30, F32)
        total[...] = jnp.zeros(total.shape, F32)
        acc[...] = jnp.zeros(acc.shape, F32)
    else:
        top[...], total[...], acc[...] = (ref[...] for ref in before)

    def qstep(qi, _):
        qs = pl.ds(pl.multiple_of(qi * QB, QB), QB)

        def kstep(kj, _):
            ks = pl.ds(pl.multiple_of(kj * KB, KB), KB)

            def work(masked):
                if masked:
                    bad = segc[ks, 0:1] != segq[0:1, qs]
                for h in range(inner // HEAD):
                    c = slice(h * HEAD, (h + 1) * HEAD)
                    s = dot(kv[ks, c], q[qs, c], NT) * CEXP
                    if masked:
                        s = jnp.where(bad, -1e30, s)
                    old = top[h : h + 1, qs]
                    new = jnp.maximum(old, jnp.max(s, 0, keepdims=True))
                    p = jnp.exp2(s - new)
                    shrink = jnp.exp2(old - new)
                    top[h : h + 1, qs] = new
                    total[h : h + 1, qs] = total[h : h + 1, qs] * shrink + jnp.sum(p, 0, keepdims=True)
                    acc[c, qs] = acc[c, qs] * shrink + dot(vt[c, ks], p.astype(LOW), NN)

            visit(info, qrow, krow, qi, kj, work)
            return 0

        lax.fori_loop(0, kv.shape[0] // KB, kstep, 0)
        return 0

    lax.fori_loop(0, q.shape[0] // QB, qstep, 0)
    if last:
        for h in range(inner // HEAD):
            c = slice(h * HEAD, (h + 1) * HEAD)
            out_t[c, :] = acc[c, :] / total[h : h + 1, :]
            lse[h : h + 1, :] = top[h : h + 1, :] + jnp.log(total[h : h + 1, :]) * LOG2E
        natural = out_t[...].T.astype(LOW)
        rows = contexts[0].shape[0]
        for i in range(4):
            contexts[i][...] = natural[i * rows : (i + 1) * rows, :]


def attend(first, last, gather, b, t, batch, inner, info, segs, pieces, more):
    rows, width = pieces[-1].shape[-2:]
    rows = rows if len(pieces) == 1 else 4 * rows // batch
    stats = [((8, rows), F32), ((8, rows), F32), ((inner, rows), F32)]
    outs = []
    if gather:
        outs += [struct((width, inner), LOW), struct((width, 2 * inner), LOW)]
    outs.append(struct((rows, 2 * inner), LOW))
    if first:
        outs.append(struct((rows, inner), LOW))
    if last:
        outs += [struct((rows // 4, inner), LOW)] * 4 + [struct((inner, rows), F32), struct((8, rows), F32)]
    else:
        outs += [struct(*item) for item in stats]
    scratch = [pltpu.VMEM(*item) for item in stats] if last else []
    scratch += [pltpu.VMEM((rows, width), LOW), pltpu.VMEM((inner, rows), LOW)]
    scratch += [pltpu.VMEM((8, rows), jnp.int32), pltpu.VMEM((rows, 128), jnp.int32)]
    body = functools.partial(fwd_body, first, last, gather, b, b, t * batch + b, len(pieces))
    return call(body, [info, segs, *pieces, *more], outs, scratch, 24, 9)


def bwd_body(first, last, add, again, b, qrow, krow, count, info, segs, *refs):
    refs = list(refs)
    pieces = [refs.pop(0) for _ in range(count)]
    back = [refs.pop(0) for _ in range(4)]
    wkv, q, kv, lse, extra = (refs.pop(0) for _ in range(5))
    if not first:
        dq_before = refs.pop(0)
    if add:
        gkv_before, vsum_before = refs.pop(0), refs.pop(0)
    if last:
        wq = refs.pop(0)
    if again:
        gq_before, qsum_before = refs.pop(0), refs.pop(0)
    keep, send, gkv, vsum = (refs.pop(0) for _ in range(4))
    if first:
        delta = refs.pop(0)
    else:
        delta = extra
    if last:
        gq, qsum = refs.pop(0), refs.pop(0)
    dq = refs.pop(0)
    hidden, do, kt, segq, segc, dk, dv, dkv = refs
    inner = q.shape[1]
    load_hidden(info, b, hidden, pieces)
    fill(do, back)
    load_segments(info, qrow, krow, segs, segq, segc)
    kt[...] = kv[:, :inner].astype(F32).T.astype(LOW)
    if first:
        product = do[...].astype(F32).T * extra[...]
        delta[...] = jnp.zeros(delta.shape, F32)
        for h in range(inner // HEAD):
            delta[h : h + 1, :] = jnp.sum(product[h * HEAD : (h + 1) * HEAD, :], 0, keepdims=True)
        dq[...] = jnp.zeros(dq.shape, F32)
    else:
        dq[...] = dq_before[...]
    dk[...] = jnp.zeros(dk.shape, F32)
    dv[...] = jnp.zeros(dv.shape, F32)

    def kstep(kj, _):
        ks = pl.ds(pl.multiple_of(kj * KB, KB), KB)

        def qstep(qi, _):
            qs = pl.ds(pl.multiple_of(qi * QB, QB), QB)

            def work(masked):
                if masked:
                    bad = segc[ks, 0:1] != segq[0:1, qs]
                for h in range(inner // HEAD):
                    c = slice(h * HEAD, (h + 1) * HEAD)
                    cv = slice(inner + h * HEAD, inner + (h + 1) * HEAD)
                    qh = q[qs, c]
                    dh = do[qs, c]
                    s = dot(kv[ks, c], qh, NT) * CEXP - lse[h : h + 1, qs]
                    if masked:
                        s = jnp.where(bad, -1e30, s)
                    p = jnp.exp2(s)
                    dp = dot(kv[ks, cv], dh, NT)
                    ds = (p * (dp - delta[h : h + 1, qs])).astype(LOW)
                    dv[ks, c] += dot(p.astype(LOW), dh, NN)
                    dk[ks, c] += dot(ds, qh, NN)
                    dq[c, qs] += dot(kt[c, ks], ds, NN)

            visit(info, qrow, krow, qi, kj, work)
            return 0

        lax.fori_loop(0, q.shape[0] // QB, qstep, 0)
        return 0

    lax.fori_loop(0, kv.shape[0] // KB, kstep, 0)
    dkv[:, :inner] = (dk[...] * SCALE).astype(LOW)
    dkv[:, inner:] = dv[...].astype(LOW)
    total = jnp.broadcast_to(jnp.sum(dv[...], 0, keepdims=True), vsum.shape)
    vsum[...] = vsum_before[...] + total if add else total
    half = keep.shape[0]
    if last:
        dq_low = (dq[...] * SCALE).T
        total = jnp.broadcast_to(jnp.sum(dq_low, 0, keepdims=True), qsum.shape)
        qsum[...] = qsum_before[...] + total if again else total
        dq_low = dq_low.astype(LOW)
        value = dot((dq[...] * SCALE).astype(LOW), hidden[...], NN)
        gq[...] = gq_before[...] + value if again else value
    for part, out in ((slice(0, half), keep), (slice(half, 2 * half), send)):
        value = dot(dkv[part, :], wkv[...], NT)
        if last:
            value = value + dot(dq_low[part, :], wq[...], NT)
        out[...] = value.astype(LOW)
    parts = [(dk[...] * SCALE).T.astype(LOW), dv[...].T.astype(LOW)]
    for i in range(2):
        rows = slice(i * inner, (i + 1) * inner)
        value = dot(parts[i], hidden[...], NN)
        gkv[rows, :] = gkv_before[rows, :] + value if add else value


def attend_back(first, last, b, t, batch, info, segs, pieces, back, wkv, q, kv, lse, extra, dq, sums, wq, more):
    rows, inner = q.shape
    width = wkv.shape[0]
    outs = [struct((rows // 2, width), LOW)] * 2 + [struct((2 * inner, width), F32), struct((8, inner), F32)]
    if first:
        outs.append(struct((8, rows), F32))
    if last:
        outs += [struct((inner, width), F32), struct((8, inner), F32)]
    scratch = []
    if last:
        scratch.append(pltpu.VMEM((inner, rows), F32))
    else:
        outs.append(struct((inner, rows), F32))
    scratch += [
        pltpu.VMEM((rows, width), LOW),
        pltpu.VMEM((rows, inner), LOW),
        pltpu.VMEM((inner, rows), LOW),
        pltpu.VMEM((8, rows), jnp.int32),
        pltpu.VMEM((rows, 128), jnp.int32),
        pltpu.VMEM((rows, inner), F32),
        pltpu.VMEM((rows, inner), F32),
        pltpu.VMEM((rows, 2 * inner), LOW),
    ]
    ins = [info, segs, *pieces, *back, wkv, q, kv, lse, extra]
    ins += [] if first else [dq]
    ins += [*sums]
    ins += [wq, *more] if last else []
    body = functools.partial(
        bwd_body, first, last, len(sums) > 0, last and len(more) > 0, b, b, t * batch + b, len(pieces)
    )
    return call(body, ins, outs, scratch, 28, 12)


def assemble_body(info, *refs):
    parts, out = refs[:4], refs[-1]
    share = parts[0].shape[0]
    for i in range(4):
        out[0, chunk_rows(info, i, share), :] = parts[i][...].astype(out.dtype)


def assemble(info, parts, batch, share, dtype, at, whole):
    count, width = parts[0].shape[0] // share, parts[0].shape[1]
    specs = [SMEM] + [pl.BlockSpec((share, width), lambda i: (i, 0))] * 4
    ins = [info, *parts]
    if whole is not None:
        ins.append(whole)
        specs.append(pl.BlockSpec(memory_space=pl.ANY))
    return pl.pallas_call(
        assemble_body,
        grid=(count,),
        cost_estimate=pl.CostEstimate(flops=int(2e9), bytes_accessed=1 << 20, transcendentals=0),
        out_shape=struct((batch, 4 * share, width), dtype),
        in_specs=specs,
        out_specs=pl.BlockSpec((1, 4 * share, width), lambda i: (i + at, 0, 0)),
        input_output_aliases={} if whole is None else {5: 0},
        compiler_params=pltpu.CompilerParams(vmem_limit_bytes=16 * 2**20),
    )(*ins)


def finish_body(info, gq, gkv, *refs):
    outs, whole = refs[:-1], refs[-1]
    inner = gq.shape[0]
    whole[...] = jnp.zeros(whole.shape, F32)
    whole[:inner, :] = gq[...]
    whole[inner : 3 * inner, :] = gkv[...]
    rows = outs[0].shape[0]
    if len(outs) == 1:
        outs[0][...] = whole[...].T.astype(LOW)
        return
    first, second = whole[:, :rows].T.astype(LOW), whole[:, rows:].T.astype(LOW)
    low = info[1] == 0
    outs[0][...] = jnp.where(low, first, second)
    outs[1][...] = jnp.where(low, second, first)


def finish_qkv(halves, info, gq, gkv):
    inner, width = gq.shape
    columns = -(-3 * inner // 128) * 128
    rows = width // 2 if halves else width
    outs = [struct((rows, columns), LOW)] * (2 if halves else 1)
    return call(finish_body, [info, gq, gkv], outs, [pltpu.VMEM((columns, width), F32)], 20, 2)


def rows_body(halves, batch, info, *refs):
    refs = list(refs)
    take = lambda count: [refs.pop(0) for _ in range(count)]
    ctx_in = take(4 * batch)
    hidden, cot, vec, bias = take(4)
    low_w, high_w = take(4), take(4)
    out_low, grad_first, sums, bias_sums = take(4)
    back = take(4 * batch)
    acts, pres, ctxs = take(4), take(4), take(4)
    nl_t, dl_t, al_t = take(3)
    slopes = take(4)
    width = hidden.shape[1]
    half = width // 2
    units, inner = bias.shape[1], ctxs[0].shape[1]
    up, down, proj = slice(0, units), slice(units, 2 * units), slice(2 * units, 2 * units + inner)

    def swapped(value):
        if not halves:
            return value
        turned = jnp.concatenate([value[:, half:], value[:, :half]], 1)
        return jnp.where(info[1] == 1, turned, value)

    def into(value, r, cols):
        return dot(value[:, :half], low_w[r][:, cols], NN) + dot(value[:, half:], high_w[r][:, cols], NN)

    def out_of(value, r, cols):
        return jnp.concatenate([dot(value, low_w[r][:, cols], NT), dot(value, high_w[r][:, cols], NT)], 1)

    def norm(value):
        center = value - jnp.mean(value, -1, keepdims=True)
        inverse = lax.rsqrt(jnp.mean(center * center, -1, keepdims=True) + EPS)
        return center * inverse, inverse

    def norm_back(grad, unit, inverse):
        shared = jnp.mean(grad, -1, keepdims=True)
        return inverse * (grad - shared - unit * jnp.mean(grad * unit, -1, keepdims=True))

    attn = None
    for r in range(4):
        fill(ctxs[r], [ctx_in[b * 4 + r] for b in range(batch)])
        part = out_of(ctxs[r][...], r, proj)
        attn = part if attn is None else attn + part
    unit_one, inverse_one = norm(hidden[...].astype(F32) + swapped(attn) + vec[0:1, :])
    normed = unit_one * vec[1:2, :] + vec[2:3, :]
    normed_sw = swapped(normed)
    nl_t[...] = normed_sw.T.astype(LOW)
    normed_low = normed_sw.astype(LOW)
    total = None
    for r in range(4):
        pre = into(normed_low, r, up) + bias[r : r + 1, :]
        gate = 0.5 + 0.5 * lax.erf(pre * 0.7071067811865476)
        acts[r][...] = (pre * gate).astype(LOW)
        slopes[r][...] = gate + pre * (0.3989422804014327 * jnp.exp(-0.5 * pre * pre))
        part = out_of(acts[r][...], r, down)
        total = part if total is None else total + part
    unit_two, inverse_two = norm(normed + swapped(total) + vec[3:4, :])
    out_low[...] = (unit_two * vec[4:5, :] + vec[5:6, :]).astype(LOW)
    cotangent = cot[...].astype(F32)
    grad_second = norm_back(cotangent * vec[4:5, :], unit_two, inverse_two)
    sums[...] = jnp.zeros(sums.shape, F32)
    sums[0:1, :] = jnp.sum(grad_second, 0, keepdims=True)
    sums[1:2, :] = jnp.sum(cotangent * unit_two, 0, keepdims=True)
    sums[2:3, :] = jnp.sum(cotangent, 0, keepdims=True)
    second_sw = swapped(grad_second)
    dl_t[...] = second_sw.T.astype(LOW)
    down_low = second_sw.astype(LOW)
    total = None
    for r in range(4):
        pre_low = (into(down_low, r, down) * slopes[r][...]).astype(LOW)
        pres[r][...] = pre_low
        bias_sums[r : r + 1, :] = jnp.sum(pre_low.astype(F32), 0, keepdims=True)
        part = out_of(pre_low, r, up)
        total = part if total is None else total + part
    grad_normed = grad_second + swapped(total)
    first = norm_back(grad_normed * vec[1:2, :], unit_one, inverse_one)
    grad_first[...] = first
    sums[3:4, :] = jnp.sum(first, 0, keepdims=True)
    sums[4:5, :] = jnp.sum(grad_normed * unit_one, 0, keepdims=True)
    sums[5:6, :] = jnp.sum(grad_normed, 0, keepdims=True)
    first_sw = swapped(first)
    al_t[...] = first_sw.T.astype(LOW)
    attn_low = first_sw.astype(LOW)
    share = back[0].shape[0]
    for r in range(4):
        value = into(attn_low, r, proj).astype(LOW)
        for b in range(batch):
            back[b * 4 + r][...] = value[b * share : (b + 1) * share, :]


def own_rows_pass(halves, batch, flag, ctx, hidden, cot, vec, bias, low_w, high_w):
    rows, width = hidden.shape
    share, inner = ctx[0].shape
    units = bias.shape[1]
    outs = [struct((rows, width), LOW), struct((rows, width), F32), struct((8, width), F32), struct((4, units), F32)]
    outs += [struct((share, inner), LOW)] * (4 * batch)
    outs += [struct((rows, units), LOW)] * 8 + [struct((rows, inner), LOW)] * 4
    outs += [struct((width, rows), LOW)] * 3
    ins = [flag, *ctx, hidden, cot, vec, bias, *low_w, *high_w]
    scratch = [pltpu.VMEM((rows, units), F32)] * 4
    return call(functools.partial(rows_body, halves, batch), ins, outs, scratch, 40, 26)


def grads_body(nl_t, dl_t, al_t, pre, act, ctx, out):
    units = act.shape[1]
    out[:, :units] = dot(nl_t[...], pre[...], NN).astype(LOW)
    out[:, units : 2 * units] = dot(dl_t[...], act[...], NN).astype(LOW)
    inner = ctx.shape[1]
    out[:, 2 * units : 2 * units + inner] = dot(al_t[...], ctx[...], NN).astype(LOW)
    out[:, 2 * units + inner :] = jnp.zeros((out.shape[0], out.shape[1] - 2 * units - inner), LOW)


def weight_grads(nl_t, dl_t, al_t, pre, act, ctx):
    shape = (nl_t.shape[0], -(-(2 * act.shape[1] + ctx.shape[1]) // 128) * 128)
    return call(grads_body, [nl_t, dl_t, al_t, pre, act, ctx], [struct(shape, LOW)], [], 20, 2, 0)[0]


def flip(value, axis, bit):
    size = lax.axis_size(axis)
    return lax.ppermute(value, axis, [(i, i ^ bit) for i in range(size)])


def onward(value, step=1):
    size = lax.axis_size("seq")
    return lax.ppermute(value, "seq", [(i, (i + step) % size) for i in range(size)])


def after(value, *others):
    return lax.optimization_barrier((value,) + others)[0]


def low_sum(left, right):
    return (left.astype(F32) + right.astype(F32)).astype(LOW)


def shards(
    hidden_in,
    segments,
    cotangent,
    qkv_weight,
    qv_bias,
    proj_weight,
    proj_bias,
    first_gain,
    first_shift,
    up_weight,
    up_bias,
    down_weight,
    down_bias,
    second_gain,
    second_shift,
):
    batch, local_len, width = hidden_in.shape
    inner = qkv_weight.shape[2]
    n_dp, n_seq, n_mp = lax.axis_size("dp"), lax.axis_size("seq"), lax.axis_size("mp")
    assert n_mp == 4
    d_at, s_at, m_at = lax.axis_index("dp"), lax.axis_index("seq"), lax.axis_index("mp")
    chunk_at = (m_at % 2) * 2 + m_at // 2
    share = local_len // n_mp
    shard_rows = qkv_weight.shape[0]
    halves = n_dp == 2

    def place(pieces, positions):
        whole = jnp.zeros((len(pieces),) + pieces[0].shape, pieces[0].dtype)
        for piece, position in zip(pieces, positions):
            whole = lax.dynamic_update_index_in_dim(whole, piece, position, 0)
        return whole.reshape((-1,) + pieces[0].shape[1:])

    def chunk(rows, i):
        parts = rows.reshape((4, share) + rows.shape[1:])
        return lax.dynamic_index_in_dim(parts, chunk_at ^ i, 0, keepdims=False)

    def own(rows):
        return jnp.concatenate([chunk(rows[b], 0) for b in range(batch)], 0)

    spare = jnp.zeros((shard_rows, -3 * inner % 128), LOW)
    flat_qkv = jnp.concatenate([qkv_weight.reshape(shard_rows, 3 * inner), spare], 1)
    if halves:
        pair = jnp.concatenate([flat_qkv, flip(flat_qkv, "dp", 1)], 0)
        qkv_shards = [pair] + [onward(pair, t) for t in range(1, n_seq)]
    else:
        qkv_shards = [lax.all_gather(flat_qkv, ("dp", "seq"), axis=0, tiled=True)]
    bias_q, bias_v = qv_bias[0:1], qv_bias[1:2]

    seg_all = [segments] + [onward(segments, t) for t in range(1, n_seq)]
    segs = jnp.concatenate(seg_all, 0)
    edges = segs.reshape(-1, 2, local_len // 2)[:, :, :: local_len // 2 - 1].reshape(-1)
    info = jnp.concatenate([jnp.stack([chunk_at, d_at]), edges, s_at[None]]).astype(jnp.int32)
    hidden_blocks = [[[hidden_in] for b in range(batch)]]
    own_chunks = [chunk(hidden_in[b], 0) for b in range(batch)]
    spare = jnp.zeros((shard_rows, -(2 * up_weight.shape[1] + inner) % 128), LOW)
    shard = jnp.concatenate([up_weight, down_weight, proj_weight, spare], 1)
    shard_pieces = [shard]
    for t in range(1, n_seq):
        shard_pieces.append(onward(shard_pieces[-1]))

    def share_over_mp(piece):
        across = flip(piece, "mp", 2)
        return [piece, across, flip(piece, "mp", 1), flip(across, "mp", 1)]

    own_rows = jnp.concatenate(own_chunks, 0)
    arrived = [after(own_rows, *qkv_shards)]
    for t in range(1, n_seq):
        arrived.append(onward(arrived[-1]))

    seq_whole = place(shard_pieces, [(s_at - t) % n_seq for t in range(n_seq)])

    def over_dp(block):
        if halves:
            return block, flip(block, "dp", 1)
        return tuple(jnp.split(lax.all_gather(block, "dp", axis=0, tiled=True), 2, 0))

    near_low, near_high = over_dp(seq_whole)
    far_low, far_high = over_dp(flip(seq_whole, "mp", 2))
    low_w = [near_low, far_low, flip(near_low, "mp", 1), flip(far_low, "mp", 1)]
    high_w = [near_high, far_high, flip(near_high, "mp", 1), flip(far_high, "mp", 1)]
    up_bias_row = up_bias[None, :]
    bias_far = flip(up_bias_row, "mp", 2)
    biases = jnp.concatenate([up_bias_row, bias_far, flip(up_bias_row, "mp", 1), flip(bias_far, "mp", 1)], 0)

    queries = [None] * batch
    key_values = [[None] * batch for _ in range(n_seq)]
    state = [None] * batch
    contexts = []
    lse, out_t = [None] * batch, [None] * batch
    order = [(t, b) for t in range(n_seq) for b in range(batch)]
    token = weight_q = weight_kv = None
    waits = {4: [near_high], 5: [far_low], 6: [far_high]}
    for step, (t, b) in enumerate(order):
        first, last = t == 0, t == n_seq - 1
        if b == 0 and t:
            if t == 1:
                crossed = [None, flip(after(arrived[1], token), "mp", 2)]
            across = crossed[t] if t == 1 else after(crossed[t], token)
            pieces = [arrived[t], crossed[t], flip(arrived[t], "mp", 1), flip(across, "mp", 1)]
            hidden_blocks.append([pieces] * batch)
            if t < n_seq - 1:
                crossed.append(flip(arrived[t + 1], "mp", 2))
        gather = len(qkv_shards) if step == 0 else 0
        more = (*qkv_shards, bias_v) if gather else (weight_kv, bias_v)
        if first:
            more += (bias_q,) if gather else (weight_q, bias_q)
        else:
            more += (queries[b], *state[b])
        held = info if token is None else after(info, token, *waits.get(step, []))
        outs = list(attend(first, last, gather, b, t, batch, inner, held, segs, hidden_blocks[t][b], more))
        if gather:
            weight_q, weight_kv = outs.pop(0), outs.pop(0)
        token = key_values[t][b] = outs.pop(0)
        if first:
            queries[b] = outs.pop(0)
        if last:
            contexts.append([outs[0]] + [flip(outs[i], "mp", FLIP[i]) for i in range(1, 4)])
            out_t[b], lse[b] = outs[4:]
        else:
            state[b] = outs

    vec = jnp.stack([proj_bias, first_gain, first_shift, down_bias, second_gain, second_shift])
    outs = list(
        own_rows_pass(
            halves, batch, info, [c for cs in contexts for c in cs],
            own_rows, own(cotangent), vec, biases, low_w, high_w,
        )
    )
    out_own, grad_first, sums, bias_sums = outs[:4]
    back, outs = outs[4 : 4 + 4 * batch], outs[4 + 4 * batch :]
    acts, pres, ctxs, transposed = outs[:4], outs[4:8], outs[8:12], outs[12:]
    back = [
        [back[b * 4]] + [flip(back[b * 4 + i], "mp", FLIP[i]) for i in range(1, 4)] for b in range(batch)
    ]
    grads = [None] * 4
    for i in (2, 3, 0, 1):
        grads[i] = weight_grads(*transposed, pres[i], acts[i], ctxs[i])

    def ring_sum(rows):
        parts = rows.reshape((n_seq, -1) + rows.shape[1:])
        total = None
        hops = []
        for t in range(1, n_seq + 1):
            part = lax.dynamic_index_in_dim(parts, (s_at - t) % n_seq, 0, keepdims=False).astype(F32)
            if total is not None:
                part = part + onward(total).astype(F32)
            total = part.astype(LOW)
            hops.append(total)
        return hops[:-1] + [part]

    def dp_sum(mine, theirs):
        if halves:
            rows = mine.shape[0] // 2
            sent = flip(low_sum(mine[rows:], theirs[rows:]), "dp", 1).astype(F32)
            return (mine[:rows].astype(F32) + theirs[:rows].astype(F32) + sent).astype(LOW)
        return lax.psum_scatter(low_sum(mine, theirs), "dp", scatter_dimension=0, tiled=True)

    near_in, far_in = flip(grads[2], "mp", 1), flip(grads[3], "mp", 1)
    near_half, far_half = dp_sum(grads[0], near_in), dp_sum(grads[1], far_in)
    near_hops, far_hops = ring_sum(near_half), ring_sum(far_half)
    owned = near_hops[-1] + flip(far_hops[-1].astype(LOW), "mp", 2).astype(F32)
    units = up_weight.shape[1]
    up_owned, down_owned = owned[:, :units], owned[:, units : 2 * units]
    proj_owned = owned[:, 2 * units : 2 * units + inner]

    layer_out = assemble(info, share_over_mp(out_own), batch, share, LOW, 0, None)

    small = jnp.concatenate([sums, bias_sums], 0)
    far_small = flip(small, "mp", 2)
    common = small[:8] + far_small[:8]
    near_bias, next_bias = small[8:9] + far_small[9:10], small[10:11] + far_small[11:12]
    small = jnp.concatenate([common, next_bias], 0)
    far_small = flip(small, "mp", 1)
    small = jnp.concatenate([common + far_small[:8], near_bias + far_small[8:]], 0)

    hops = []
    for axis, size in (("dp", n_dp), ("seq", n_seq)):
        bit = 1
        while bit < size:
            hops.append((axis, bit))
            bit *= 2

    def over_groups(value):
        for axis, bit in hops:
            value = value + flip(value, axis, bit)
        return value

    sums, more = (), ()
    input_grad = None
    theirs_of, across_of, passing_of = [], [], []
    waits = {
        1: [near_in, far_in],
        2: [layer_out],
        4: [near_half],
        5: [far_half, near_hops[0]],
        6: [near_hops[1], far_hops[0]],
        7: [near_hops[2], far_hops[1]],
    }
    for b in range(batch):
        dq = None
        extra = out_t[b]
        passing = None
        for t in list(range(1, n_seq)) + [0]:
            first, last = t == 1, t == 0
            step = len(theirs_of)
            waiting = waits.get(step, [])
            waiting = waiting + theirs_of[max(step - 2, 0) : max(step - 1, 0)]
            waiting = waiting + across_of[max(step - 3, 0) : max(step - 2, 0)]
            lag = 2 if step == batch * n_seq - 1 else 3
            waiting = waiting + passing_of[max(step - lag, 0) : max(step - lag + 1, 0)]
            held = after(info, *waiting) if waiting else info
            outs = list(
                attend_back(
                    first, last, b, t, batch, held, segs, hidden_blocks[t][b], back[b], weight_kv,
                    queries[b], key_values[t][b], lse[b], extra, dq, sums, weight_q, more,
                )
            )
            keep, send = outs[:2]
            if step and step <= len(hops):
                axis, bit = hops[step - 1]
                small = small + flip(after(small, keep), axis, bit)
            sums = outs[2:4]
            if first:
                extra = outs[4]
            if last:
                more = outs[4:6]
            else:
                dq = outs[-1]
            theirs = flip(send, "mp", 1)
            theirs_of.append(theirs)
            across = flip(low_sum(keep[share:], theirs[share:]), "mp", 2)
            across_of.append(across)
            rows = keep[:share].astype(F32) + theirs[:share].astype(F32) + across.astype(F32)
            if passing is not None:
                rows = rows + onward(passing).astype(F32)
            passing = rows.astype(LOW)
            passing_of.append(passing)
        piece = (grad_first[b * share : (b + 1) * share] + rows).astype(LOW)
        input_grad = assemble(info, share_over_mp(piece), batch, share, F32, b, input_grad)
    for axis, bit in hops[batch * n_seq - 1 :]:
        small = small + flip(small, axis, bit)
    norm_small, up_bias_grad = small[:8], small[8]
    gq, q_sum = more
    gkv, v_sum = sums
    finished = finish_qkv(halves, info, gq, gkv)
    if halves:
        grad_qkv = low_sum(finished[0], flip(after(finished[1], theirs_of[-1]), "dp", 1))
    else:
        grad_qkv = lax.psum_scatter(finished[0], "dp", scatter_dimension=0, tiled=True)
    qkv_owned = ring_sum(grad_qkv)[-1][:, : 3 * inner].reshape(shard_rows, 3, inner)
    qv_bias_grad = over_groups(after(jnp.concatenate([q_sum[:1], v_sum[:1]], 0), theirs_of[-1]))
    return (
        layer_out,
        input_grad,
        qkv_owned,
        qv_bias_grad,
        proj_owned,
        norm_small[3],
        norm_small[4],
        norm_small[5],
        up_owned,
        up_bias_grad,
        down_owned,
        norm_small[0],
        norm_small[1],
        norm_small[2],
    )


def solution(mesh):
    in_specs = (
        P("dp", "seq", None),
        P("dp", "seq"),
        P("dp", "seq", None),
        P(("dp", "seq"), None, "mp"),
        P(None, "mp"),
        P(("dp", "seq"), "mp"),
        P(),
        P(),
        P(),
        P(("dp", "seq"), "mp"),
        P("mp"),
        P(("dp", "seq"), "mp"),
        P(),
        P(),
        P(),
    )
    out_specs = (
        P("dp", "seq", None),
        P("dp", "seq", None),
        P(("dp", "seq"), None, "mp"),
        P(None, "mp"),
        P(("dp", "seq"), "mp"),
        P(),
        P(),
        P(),
        P(("dp", "seq"), "mp"),
        P("mp"),
        P(("dp", "seq"), "mp"),
        P(),
        P(),
        P(),
    )
    return jax.shard_map(shards, mesh=mesh, in_specs=in_specs, out_specs=out_specs, check_vma=False)
```

```python
import functools

import jax
import jax.numpy as jnp
from jax import lax
from jax.experimental import pallas as pl
from jax.experimental.pallas import tpu as pltpu
from jax.sharding import PartitionSpec as P

HEAD = 64
EPS = 1e-06
SCALE = HEAD**-0.5
LOG2E = 1.4426950408889634
CEXP = LOG2E * SCALE
QB = 512
KB = 512
NT = (((1,), (1,)), ((), ()))
NN = (((1,), (0,)), ((), ()))
VMEM = pl.BlockSpec(memory_space=pltpu.VMEM)
SMEM = pl.BlockSpec(memory_space=pltpu.SMEM)
LOW = jnp.bfloat16
F32 = jnp.float32
FLIP = (0, 2, 1, 3)


def dot(left, right, dims):
    return lax.dot_general(left, right, dims, preferred_element_type=F32)


def struct(shape, dtype):
    return jax.ShapeDtypeStruct(shape, dtype)


def call(body, ins, outs, scratch, mib, micros, scalars=1):
    return pl.pallas_call(
        body,
        cost_estimate=pl.CostEstimate(
            flops=int(micros * 1.1e9), bytes_accessed=1 << 20, transcendentals=0
        ),
        out_shape=tuple(outs),
        in_specs=[SMEM] * scalars + [VMEM] * (len(ins) - scalars),
        out_specs=(VMEM,) * len(outs),
        scratch_shapes=scratch,
        compiler_params=pltpu.CompilerParams(vmem_limit_bytes=mib * 2**20),
    )(*ins)


def visit(info, qrow, krow, qi, kj, work):
    qat = 2 + 4 * qrow + 2 * (qi ^ (info[0] // 2))
    kat = 2 + 4 * krow + 2 * (kj ^ (info[0] // 2))
    qlo, qhi, klo, khi = info[qat], info[qat + 1], info[kat], info[kat + 1]
    overlap = (qlo <= khi) & (klo <= qhi)
    pure = (qlo == qhi) & (klo == khi) & (qlo == klo)
    pl.when(pure)(lambda: work(False))
    pl.when(overlap & jnp.logical_not(pure))(lambda: work(True))


def fill(target, pieces):
    rows = pieces[0].shape[0]
    for i, piece in enumerate(pieces):
        target[i * rows : (i + 1) * rows, :] = piece[...]


def chunk_rows(info, i, share):
    return pl.ds(pl.multiple_of((info[0] ^ i) * share, share), share)


def load_hidden(info, b, target, pieces):
    share = target.shape[0] // 4
    if len(pieces) > 1:
        for i in range(4):
            target[i * share : (i + 1) * share, :] = pieces[i][b * share : (b + 1) * share, :]
        return
    for i in range(4):
        target[i * share : (i + 1) * share, :] = pieces[0][b, chunk_rows(info, i, share), :]


def load_segments(info, qrow, krow, segs, segq, segc):
    share = segq.shape[1] // 4
    for i in range(4):
        cols = chunk_rows(info, i, share)
        own = slice(i * share, (i + 1) * share)
        segq[:, own] = jnp.broadcast_to(segs[qrow : qrow + 1, cols], (8, share))
        segc[own, :] = jnp.broadcast_to(segs[krow : krow + 1, cols], (128, share)).astype(F32).T.astype(jnp.int32)


def fwd_body(first, last, gather, b, qrow, krow, count, info, segs, *refs):
    refs = list(refs)
    pieces = [refs.pop(0) for _ in range(count)]
    if gather:
        shards = [refs.pop(0) for _ in range(gather)]
        vbias = refs.pop(0)
    else:
        wkv, vbias = refs.pop(0), refs.pop(0)
    if first:
        if not gather:
            wq = refs.pop(0)
        qbias = refs.pop(0)
        before = None
    else:
        q = refs.pop(0)
        before = [refs.pop(0) for _ in range(3)]
    if gather:
        wq, wkv = refs.pop(0), refs.pop(0)
    kv = refs.pop(0)
    if first:
        q = refs.pop(0)
    if last:
        contexts = [refs.pop(0) for _ in range(4)]
        out_t, lse = refs.pop(0), refs.pop(0)
    top, total, acc = refs.pop(0), refs.pop(0), refs.pop(0)
    hidden, vt, segq, segc = refs
    inner = q.shape[1]
    load_hidden(info, b, hidden, pieces)
    load_segments(info, qrow, krow, segs, segq, segc)
    for j in range(gather):
        parts = 1 if gather == 1 else 2
        height = shards[j].shape[0] // parts
        for y in range(parts):
            at = 0
            if parts == 2:
                back = info[info.shape[0] - 1] - j
                at = (info[1] ^ y) * gather + jnp.where(back < 0, back + gather, back)
            rows = pl.ds(pl.multiple_of(at * height, height), height)
            source = slice(y * height, (y + 1) * height)
            wq[rows, :] = shards[j][source, :inner]
            wkv[rows, :] = shards[j][source, inner : 3 * inner]
    value = dot(hidden[...], wkv[...], NN)
    kv[:, :inner] = value[:, :inner].astype(LOW)
    value = value[:, inner:] + vbias[...]
    kv[:, inner:] = value.astype(LOW)
    vt[...] = value.T.astype(LOW)
    if first:
        q[...] = (dot(hidden[...], wq[...], NN) + qbias[...]).astype(LOW)
        top[...] = jnp.full(top.shape, -1e30, F32)
        total[...] = jnp.zeros(total.shape, F32)
        acc[...] = jnp.zeros(acc.shape, F32)
    else:
        top[...], total[...], acc[...] = (ref[...] for ref in before)

    def qstep(qi, _):
        qs = pl.ds(pl.multiple_of(qi * QB, QB), QB)

        def kstep(kj, _):
            ks = pl.ds(pl.multiple_of(kj * KB, KB), KB)

            def work(masked):
                if masked:
                    bad = segc[ks, 0:1] != segq[0:1, qs]
                for h in range(inner // HEAD):
                    c = slice(h * HEAD, (h + 1) * HEAD)
                    s = dot(kv[ks, c], q[qs, c], NT) * CEXP
                    if masked:
                        s = jnp.where(bad, -1e30, s)
                    old = top[h : h + 1, qs]
                    new = jnp.maximum(old, jnp.max(s, 0, keepdims=True))
                    p = jnp.exp2(s - new)
                    shrink = jnp.exp2(old - new)
                    top[h : h + 1, qs] = new
                    total[h : h + 1, qs] = total[h : h + 1, qs] * shrink + jnp.sum(p, 0, keepdims=True)
                    acc[c, qs] = acc[c, qs] * shrink + dot(vt[c, ks], p.astype(LOW), NN)

            visit(info, qrow, krow, qi, kj, work)
            return 0

        lax.fori_loop(0, kv.shape[0] // KB, kstep, 0)
        return 0

    lax.fori_loop(0, q.shape[0] // QB, qstep, 0)
    if last:
        for h in range(inner // HEAD):
            c = slice(h * HEAD, (h + 1) * HEAD)
            out_t[c, :] = acc[c, :] / total[h : h + 1, :]
            lse[h : h + 1, :] = top[h : h + 1, :] + jnp.log(total[h : h + 1, :]) * LOG2E
        natural = out_t[...].T.astype(LOW)
        rows = contexts[0].shape[0]
        for i in range(4):
            contexts[i][...] = natural[i * rows : (i + 1) * rows, :]


def attend(first, last, gather, b, t, batch, inner, info, segs, pieces, more):
    rows, width = pieces[-1].shape[-2:]
    rows = rows if len(pieces) == 1 else 4 * rows // batch
    stats = [((8, rows), F32), ((8, rows), F32), ((inner, rows), F32)]
    outs = []
    if gather:
        outs += [struct((width, inner), LOW), struct((width, 2 * inner), LOW)]
    outs.append(struct((rows, 2 * inner), LOW))
    if first:
        outs.append(struct((rows, inner), LOW))
    if last:
        outs += [struct((rows // 4, inner), LOW)] * 4 + [struct((inner, rows), F32), struct((8, rows), F32)]
    else:
        outs += [struct(*item) for item in stats]
    scratch = [pltpu.VMEM(*item) for item in stats] if last else []
    scratch += [pltpu.VMEM((rows, width), LOW), pltpu.VMEM((inner, rows), LOW)]
    scratch += [pltpu.VMEM((8, rows), jnp.int32), pltpu.VMEM((rows, 128), jnp.int32)]
    body = functools.partial(fwd_body, first, last, gather, b, b, t * batch + b, len(pieces))
    return call(body, [info, segs, *pieces, *more], outs, scratch, 24, 9)


def bwd_body(first, last, add, again, b, qrow, krow, count, info, segs, *refs):
    refs = list(refs)
    pieces = [refs.pop(0) for _ in range(count)]
    back = [refs.pop(0) for _ in range(4)]
    wkv, q, kv, lse, extra = (refs.pop(0) for _ in range(5))
    if not first:
        dq_before = refs.pop(0)
    if add:
        gkv_before, vsum_before = refs.pop(0), refs.pop(0)
    if last:
        wq = refs.pop(0)
    if again:
        gq_before, qsum_before = refs.pop(0), refs.pop(0)
    keep, send, gkv, vsum = (refs.pop(0) for _ in range(4))
    if first:
        delta = refs.pop(0)
    else:
        delta = extra
    if last:
        gq, qsum = refs.pop(0), refs.pop(0)
    dq = refs.pop(0)
    hidden, do, kt, segq, segc, dk, dv, dkv = refs
    inner = q.shape[1]
    load_hidden(info, b, hidden, pieces)
    fill(do, back)
    load_segments(info, qrow, krow, segs, segq, segc)
    kt[...] = kv[:, :inner].astype(F32).T.astype(LOW)
    if first:
        product = do[...].astype(F32).T * extra[...]
        delta[...] = jnp.zeros(delta.shape, F32)
        for h in range(inner // HEAD):
            delta[h : h + 1, :] = jnp.sum(product[h * HEAD : (h + 1) * HEAD, :], 0, keepdims=True)
        dq[...] = jnp.zeros(dq.shape, F32)
    else:
        dq[...] = dq_before[...]
    dk[...] = jnp.zeros(dk.shape, F32)
    dv[...] = jnp.zeros(dv.shape, F32)

    def kstep(kj, _):
        ks = pl.ds(pl.multiple_of(kj * KB, KB), KB)

        def qstep(qi, _):
            qs = pl.ds(pl.multiple_of(qi * QB, QB), QB)

            def work(masked):
                if masked:
                    bad = segc[ks, 0:1] != segq[0:1, qs]
                for h in range(inner // HEAD):
                    c = slice(h * HEAD, (h + 1) * HEAD)
                    cv = slice(inner + h * HEAD, inner + (h + 1) * HEAD)
                    qh = q[qs, c]
                    dh = do[qs, c]
                    s = dot(kv[ks, c], qh, NT) * CEXP - lse[h : h + 1, qs]
                    if masked:
                        s = jnp.where(bad, -1e30, s)
                    p = jnp.exp2(s)
                    dp = dot(kv[ks, cv], dh, NT)
                    ds = (p * (dp - delta[h : h + 1, qs])).astype(LOW)
                    dv[ks, c] += dot(p.astype(LOW), dh, NN)
                    dk[ks, c] += dot(ds, qh, NN)
                    dq[c, qs] += dot(kt[c, ks], ds, NN)

            visit(info, qrow, krow, qi, kj, work)
            return 0

        lax.fori_loop(0, q.shape[0] // QB, qstep, 0)
        return 0

    lax.fori_loop(0, kv.shape[0] // KB, kstep, 0)
    dkv[:, :inner] = (dk[...] * SCALE).astype(LOW)
    dkv[:, inner:] = dv[...].astype(LOW)
    total = jnp.broadcast_to(jnp.sum(dv[...], 0, keepdims=True), vsum.shape)
    vsum[...] = vsum_before[...] + total if add else total
    half = keep.shape[0]
    if last:
        dq_low = (dq[...] * SCALE).T
        total = jnp.broadcast_to(jnp.sum(dq_low, 0, keepdims=True), qsum.shape)
        qsum[...] = qsum_before[...] + total if again else total
        dq_low = dq_low.astype(LOW)
        value = dot((dq[...] * SCALE).astype(LOW), hidden[...], NN)
        gq[...] = gq_before[...] + value if again else value
    for part, out in ((slice(0, half), keep), (slice(half, 2 * half), send)):
        value = dot(dkv[part, :], wkv[...], NT)
        if last:
            value = value + dot(dq_low[part, :], wq[...], NT)
        out[...] = value.astype(LOW)
    parts = [(dk[...] * SCALE).T.astype(LOW), dv[...].T.astype(LOW)]
    for i in range(2):
        rows = slice(i * inner, (i + 1) * inner)
        value = dot(parts[i], hidden[...], NN)
        gkv[rows, :] = gkv_before[rows, :] + value if add else value


def attend_back(first, last, b, t, batch, info, segs, pieces, back, wkv, q, kv, lse, extra, dq, sums, wq, more):
    rows, inner = q.shape
    width = wkv.shape[0]
    outs = [struct((rows // 2, width), LOW)] * 2 + [struct((2 * inner, width), F32), struct((8, inner), F32)]
    if first:
        outs.append(struct((8, rows), F32))
    if last:
        outs += [struct((inner, width), F32), struct((8, inner), F32)]
    scratch = []
    if last:
        scratch.append(pltpu.VMEM((inner, rows), F32))
    else:
        outs.append(struct((inner, rows), F32))
    scratch += [
        pltpu.VMEM((rows, width), LOW),
        pltpu.VMEM((rows, inner), LOW),
        pltpu.VMEM((inner, rows), LOW),
        pltpu.VMEM((8, rows), jnp.int32),
        pltpu.VMEM((rows, 128), jnp.int32),
        pltpu.VMEM((rows, inner), F32),
        pltpu.VMEM((rows, inner), F32),
        pltpu.VMEM((rows, 2 * inner), LOW),
    ]
    ins = [info, segs, *pieces, *back, wkv, q, kv, lse, extra]
    ins += [] if first else [dq]
    ins += [*sums]
    ins += [wq, *more] if last else []
    body = functools.partial(
        bwd_body, first, last, len(sums) > 0, last and len(more) > 0, b, b, t * batch + b, len(pieces)
    )
    return call(body, ins, outs, scratch, 28, 12)


def assemble_body(info, *refs):
    parts, out = refs[:4], refs[-1]
    share = parts[0].shape[0]
    for i in range(4):
        out[0, chunk_rows(info, i, share), :] = parts[i][...].astype(out.dtype)


def assemble(info, parts, batch, share, dtype, at, whole):
    count, width = parts[0].shape[0] // share, parts[0].shape[1]
    specs = [SMEM] + [pl.BlockSpec((share, width), lambda i: (i, 0))] * 4
    ins = [info, *parts]
    if whole is not None:
        ins.append(whole)
        specs.append(pl.BlockSpec(memory_space=pl.ANY))
    return pl.pallas_call(
        assemble_body,
        grid=(count,),
        cost_estimate=pl.CostEstimate(flops=int(2e9), bytes_accessed=1 << 20, transcendentals=0),
        out_shape=struct((batch, 4 * share, width), dtype),
        in_specs=specs,
        out_specs=pl.BlockSpec((1, 4 * share, width), lambda i: (i + at, 0, 0)),
        input_output_aliases={} if whole is None else {5: 0},
        compiler_params=pltpu.CompilerParams(vmem_limit_bytes=16 * 2**20),
    )(*ins)


def finish_body(info, gq, gkv, *refs):
    outs, whole = refs[:-1], refs[-1]
    inner = gq.shape[0]
    whole[...] = jnp.zeros(whole.shape, F32)
    whole[:inner, :] = gq[...]
    whole[inner : 3 * inner, :] = gkv[...]
    rows = outs[0].shape[0]
    if len(outs) == 1:
        outs[0][...] = whole[...].T.astype(LOW)
        return
    first, second = whole[:, :rows].T.astype(LOW), whole[:, rows:].T.astype(LOW)
    low = info[1] == 0
    outs[0][...] = jnp.where(low, first, second)
    outs[1][...] = jnp.where(low, second, first)


def finish_qkv(halves, info, gq, gkv):
    inner, width = gq.shape
    columns = -(-3 * inner // 128) * 128
    rows = width // 2 if halves else width
    outs = [struct((rows, columns), LOW)] * (2 if halves else 1)
    return call(finish_body, [info, gq, gkv], outs, [pltpu.VMEM((columns, width), F32)], 20, 2)


def rows_body(halves, batch, info, *refs):
    refs = list(refs)
    take = lambda count: [refs.pop(0) for _ in range(count)]
    ctx_in = take(4 * batch)
    hidden, cot, vec, bias = take(4)
    low_w, high_w = take(4), take(4)
    out_low, grad_first, sums, bias_sums = take(4)
    back = take(4 * batch)
    acts, pres, ctxs = take(4), take(4), take(4)
    nl_t, dl_t, al_t = take(3)
    slopes = take(4)
    width = hidden.shape[1]
    half = width // 2
    units, inner = bias.shape[1], ctxs[0].shape[1]
    up, down, proj = slice(0, units), slice(units, 2 * units), slice(2 * units, 2 * units + inner)

    def swapped(value):
        if not halves:
            return value
        turned = jnp.concatenate([value[:, half:], value[:, :half]], 1)
        return jnp.where(info[1] == 1, turned, value)

    def into(value, r, cols):
        return dot(value[:, :half], low_w[r][:, cols], NN) + dot(value[:, half:], high_w[r][:, cols], NN)

    def out_of(value, r, cols):
        return jnp.concatenate([dot(value, low_w[r][:, cols], NT), dot(value, high_w[r][:, cols], NT)], 1)

    def norm(value):
        center = value - jnp.mean(value, -1, keepdims=True)
        inverse = lax.rsqrt(jnp.mean(center * center, -1, keepdims=True) + EPS)
        return center * inverse, inverse

    def norm_back(grad, unit, inverse):
        shared = jnp.mean(grad, -1, keepdims=True)
        return inverse * (grad - shared - unit * jnp.mean(grad * unit, -1, keepdims=True))

    attn = None
    for r in range(4):
        fill(ctxs[r], [ctx_in[b * 4 + r] for b in range(batch)])
        part = out_of(ctxs[r][...], r, proj)
        attn = part if attn is None else attn + part
    unit_one, inverse_one = norm(hidden[...].astype(F32) + swapped(attn) + vec[0:1, :])
    normed = unit_one * vec[1:2, :] + vec[2:3, :]
    normed_sw = swapped(normed)
    nl_t[...] = normed_sw.T.astype(LOW)
    normed_low = normed_sw.astype(LOW)
    total = None
    for r in range(4):
        pre = into(normed_low, r, up) + bias[r : r + 1, :]
        gate = 0.5 + 0.5 * lax.erf(pre * 0.7071067811865476)
        acts[r][...] = (pre * gate).astype(LOW)
        slopes[r][...] = gate + pre * (0.3989422804014327 * jnp.exp(-0.5 * pre * pre))
        part = out_of(acts[r][...], r, down)
        total = part if total is None else total + part
    unit_two, inverse_two = norm(normed + swapped(total) + vec[3:4, :])
    out_low[...] = (unit_two * vec[4:5, :] + vec[5:6, :]).astype(LOW)
    cotangent = cot[...].astype(F32)
    grad_second = norm_back(cotangent * vec[4:5, :], unit_two, inverse_two)
    sums[...] = jnp.zeros(sums.shape, F32)
    sums[0:1, :] = jnp.sum(grad_second, 0, keepdims=True)
    sums[1:2, :] = jnp.sum(cotangent * unit_two, 0, keepdims=True)
    sums[2:3, :] = jnp.sum(cotangent, 0, keepdims=True)
    second_sw = swapped(grad_second)
    dl_t[...] = second_sw.T.astype(LOW)
    down_low = second_sw.astype(LOW)
    total = None
    for r in range(4):
        pre_low = (into(down_low, r, down) * slopes[r][...]).astype(LOW)
        pres[r][...] = pre_low
        bias_sums[r : r + 1, :] = jnp.sum(pre_low.astype(F32), 0, keepdims=True)
        part = out_of(pre_low, r, up)
        total = part if total is None else total + part
    grad_normed = grad_second + swapped(total)
    first = norm_back(grad_normed * vec[1:2, :], unit_one, inverse_one)
    grad_first[...] = first
    sums[3:4, :] = jnp.sum(first, 0, keepdims=True)
    sums[4:5, :] = jnp.sum(grad_normed * unit_one, 0, keepdims=True)
    sums[5:6, :] = jnp.sum(grad_normed, 0, keepdims=True)
    first_sw = swapped(first)
    al_t[...] = first_sw.T.astype(LOW)
    attn_low = first_sw.astype(LOW)
    share = back[0].shape[0]
    for r in range(4):
        value = into(attn_low, r, proj).astype(LOW)
        for b in range(batch):
            back[b * 4 + r][...] = value[b * share : (b + 1) * share, :]


def own_rows_pass(halves, batch, flag, ctx, hidden, cot, vec, bias, low_w, high_w):
    rows, width = hidden.shape
    share, inner = ctx[0].shape
    units = bias.shape[1]
    outs = [struct((rows, width), LOW), struct((rows, width), F32), struct((8, width), F32), struct((4, units), F32)]
    outs += [struct((share, inner), LOW)] * (4 * batch)
    outs += [struct((rows, units), LOW)] * 8 + [struct((rows, inner), LOW)] * 4
    outs += [struct((width, rows), LOW)] * 3
    ins = [flag, *ctx, hidden, cot, vec, bias, *low_w, *high_w]
    scratch = [pltpu.VMEM((rows, units), F32)] * 4
    return call(functools.partial(rows_body, halves, batch), ins, outs, scratch, 40, 26)


def grads_body(nl_t, dl_t, al_t, pre, act, ctx, out):
    units = act.shape[1]
    out[:, :units] = dot(nl_t[...], pre[...], NN).astype(LOW)
    out[:, units : 2 * units] = dot(dl_t[...], act[...], NN).astype(LOW)
    inner = ctx.shape[1]
    out[:, 2 * units : 2 * units + inner] = dot(al_t[...], ctx[...], NN).astype(LOW)
    out[:, 2 * units + inner :] = jnp.zeros((out.shape[0], out.shape[1] - 2 * units - inner), LOW)


def weight_grads(nl_t, dl_t, al_t, pre, act, ctx):
    shape = (nl_t.shape[0], -(-(2 * act.shape[1] + ctx.shape[1]) // 128) * 128)
    return call(grads_body, [nl_t, dl_t, al_t, pre, act, ctx], [struct(shape, LOW)], [], 20, 2, 0)[0]


def flip(value, axis, bit):
    size = lax.axis_size(axis)
    return lax.ppermute(value, axis, [(i, i ^ bit) for i in range(size)])


def onward(value, step=1):
    size = lax.axis_size("seq")
    return lax.ppermute(value, "seq", [(i, (i + step) % size) for i in range(size)])


def after(value, *others):
    return lax.optimization_barrier((value,) + others)[0]


def low_sum(left, right):
    return (left.astype(F32) + right.astype(F32)).astype(LOW)


def shards(
    hidden_in,
    segments,
    cotangent,
    qkv_weight,
    qv_bias,
    proj_weight,
    proj_bias,
    first_gain,
    first_shift,
    up_weight,
    up_bias,
    down_weight,
    down_bias,
    second_gain,
    second_shift,
):
    batch, local_len, width = hidden_in.shape
    inner = qkv_weight.shape[2]
    n_dp, n_seq, n_mp = lax.axis_size("dp"), lax.axis_size("seq"), lax.axis_size("mp")
    assert n_mp == 4
    d_at, s_at, m_at = lax.axis_index("dp"), lax.axis_index("seq"), lax.axis_index("mp")
    chunk_at = (m_at % 2) * 2 + m_at // 2
    share = local_len // n_mp
    shard_rows = qkv_weight.shape[0]
    halves = n_dp == 2

    def place(pieces, positions):
        whole = jnp.zeros((len(pieces),) + pieces[0].shape, pieces[0].dtype)
        for piece, position in zip(pieces, positions):
            whole = lax.dynamic_update_index_in_dim(whole, piece, position, 0)
        return whole.reshape((-1,) + pieces[0].shape[1:])

    def chunk(rows, i):
        parts = rows.reshape((4, share) + rows.shape[1:])
        return lax.dynamic_index_in_dim(parts, chunk_at ^ i, 0, keepdims=False)

    def own(rows):
        return jnp.concatenate([chunk(rows[b], 0) for b in range(batch)], 0)

    spare = jnp.zeros((shard_rows, -3 * inner % 128), LOW)
    flat_qkv = jnp.concatenate([qkv_weight.reshape(shard_rows, 3 * inner), spare], 1)
    if halves:
        pair = jnp.concatenate([flat_qkv, flip(flat_qkv, "dp", 1)], 0)
        qkv_shards = [pair] + [onward(pair, t) for t in range(1, n_seq)]
    else:
        qkv_shards = [lax.all_gather(flat_qkv, ("dp", "seq"), axis=0, tiled=True)]
    bias_q, bias_v = qv_bias[0:1], qv_bias[1:2]

    seg_all = [segments] + [onward(segments, t) for t in range(1, n_seq)]
    segs = jnp.concatenate(seg_all, 0)
    edges = segs.reshape(-1, 2, local_len // 2)[:, :, :: local_len // 2 - 1].reshape(-1)
    info = jnp.concatenate([jnp.stack([chunk_at, d_at]), edges, s_at[None]]).astype(jnp.int32)
    hidden_blocks = [[[hidden_in] for b in range(batch)]]
    own_chunks = [chunk(hidden_in[b], 0) for b in range(batch)]
    spare = jnp.zeros((shard_rows, -(2 * up_weight.shape[1] + inner) % 128), LOW)
    shard = jnp.concatenate([up_weight, down_weight, proj_weight, spare], 1)
    shard_pieces = [shard]
    for t in range(1, n_seq):
        shard_pieces.append(onward(shard_pieces[-1]))

    def share_over_mp(piece):
        across = flip(piece, "mp", 2)
        return [piece, across, flip(piece, "mp", 1), flip(across, "mp", 1)]

    own_rows = jnp.concatenate(own_chunks, 0)
    arrived = [after(own_rows, *qkv_shards)]
    for t in range(1, n_seq):
        arrived.append(onward(arrived[-1]))

    seq_whole = place(shard_pieces, [(s_at - t) % n_seq for t in range(n_seq)])

    def over_dp(block):
        if halves:
            return block, flip(block, "dp", 1)
        return tuple(jnp.split(lax.all_gather(block, "dp", axis=0, tiled=True), 2, 0))

    near_low, near_high = over_dp(seq_whole)
    far_low, far_high = over_dp(flip(seq_whole, "mp", 2))
    low_w = [near_low, far_low, flip(near_low, "mp", 1), flip(far_low, "mp", 1)]
    high_w = [near_high, far_high, flip(near_high, "mp", 1), flip(far_high, "mp", 1)]
    up_bias_row = up_bias[None, :]
    bias_far = flip(up_bias_row, "mp", 2)
    biases = jnp.concatenate([up_bias_row, bias_far, flip(up_bias_row, "mp", 1), flip(bias_far, "mp", 1)], 0)

    queries = [None] * batch
    key_values = [[None] * batch for _ in range(n_seq)]
    state = [None] * batch
    contexts = []
    lse, out_t = [None] * batch, [None] * batch
    order = [(t, b) for t in range(n_seq) for b in range(batch)]
    token = weight_q = weight_kv = None
    waits = {1: [arrived[1]], 4: [near_high], 5: [far_low], 6: [far_high]}
    for step, (t, b) in enumerate(order):
        first, last = t == 0, t == n_seq - 1
        if b == 0 and t:
            if t == 1:
                crossed = [None, flip(arrived[1], "mp", 2)]
            across = crossed[t] if t == 1 else after(crossed[t], token)
            pieces = [arrived[t], crossed[t], flip(arrived[t], "mp", 1), flip(across, "mp", 1)]
            hidden_blocks.append([pieces] * batch)
            if t < n_seq - 1:
                crossed.append(flip(arrived[t + 1], "mp", 2))
        gather = len(qkv_shards) if step == 0 else 0
        more = (*qkv_shards, bias_v) if gather else (weight_kv, bias_v)
        if first:
            more += (bias_q,) if gather else (weight_q, bias_q)
        else:
            more += (queries[b], *state[b])
        held = info if token is None else after(info, token, *waits.get(step, []))
        outs = list(attend(first, last, gather, b, t, batch, inner, held, segs, hidden_blocks[t][b], more))
        if gather:
            weight_q, weight_kv = outs.pop(0), outs.pop(0)
        token = key_values[t][b] = outs.pop(0)
        if first:
            queries[b] = outs.pop(0)
        if last:
            contexts.append([outs[0]] + [flip(outs[i], "mp", FLIP[i]) for i in range(1, 4)])
            out_t[b], lse[b] = outs[4:]
        else:
            state[b] = outs

    vec = jnp.stack([proj_bias, first_gain, first_shift, down_bias, second_gain, second_shift])
    outs = list(
        own_rows_pass(
            halves, batch, info, [c for cs in contexts for c in cs],
            own_rows, own(cotangent), vec, biases, low_w, high_w,
        )
    )
    out_own, grad_first, sums, bias_sums = outs[:4]
    back, outs = outs[4 : 4 + 4 * batch], outs[4 + 4 * batch :]
    acts, pres, ctxs, transposed = outs[:4], outs[4:8], outs[8:12], outs[12:]
    back = [
        [back[b * 4]] + [flip(back[b * 4 + i], "mp", FLIP[i]) for i in range(1, 4)] for b in range(batch)
    ]
    grads = [None] * 4
    for i in (2, 3, 0, 1):
        grads[i] = weight_grads(*transposed, pres[i], acts[i], ctxs[i])

    def ring_sum(rows):
        parts = rows.reshape((n_seq, -1) + rows.shape[1:])
        total = None
        hops = []
        for t in range(1, n_seq + 1):
            part = lax.dynamic_index_in_dim(parts, (s_at - t) % n_seq, 0, keepdims=False).astype(F32)
            if total is not None:
                part = part + onward(total).astype(F32)
            total = part.astype(LOW)
            hops.append(total)
        return hops[:-1] + [part]

    def dp_sum(mine, theirs):
        if halves:
            rows = mine.shape[0] // 2
            sent = flip(low_sum(mine[rows:], theirs[rows:]), "dp", 1).astype(F32)
            return (mine[:rows].astype(F32) + theirs[:rows].astype(F32) + sent).astype(LOW)
        return lax.psum_scatter(low_sum(mine, theirs), "dp", scatter_dimension=0, tiled=True)

    near_in, far_in = flip(grads[2], "mp", 1), flip(grads[3], "mp", 1)
    near_half, far_half = dp_sum(grads[0], near_in), dp_sum(grads[1], far_in)
    near_hops, far_hops = ring_sum(near_half), ring_sum(far_half)
    owned = near_hops[-1] + flip(far_hops[-1].astype(LOW), "mp", 2).astype(F32)
    units = up_weight.shape[1]
    up_owned, down_owned = owned[:, :units], owned[:, units : 2 * units]
    proj_owned = owned[:, 2 * units : 2 * units + inner]

    layer_out = assemble(info, share_over_mp(out_own), batch, share, LOW, 0, None)

    small = jnp.concatenate([sums, bias_sums], 0)
    far_small = flip(small, "mp", 2)
    common = small[:8] + far_small[:8]
    near_bias, next_bias = small[8:9] + far_small[9:10], small[10:11] + far_small[11:12]
    small = jnp.concatenate([common, next_bias], 0)
    far_small = flip(small, "mp", 1)
    small = jnp.concatenate([common + far_small[:8], near_bias + far_small[8:]], 0)

    hops = []
    for axis, size in (("dp", n_dp), ("seq", n_seq)):
        bit = 1
        while bit < size:
            hops.append((axis, bit))
            bit *= 2

    def over_groups(value):
        for axis, bit in hops:
            value = value + flip(value, axis, bit)
        return value

    sums, more = (), ()
    input_grad = None
    theirs_of, across_of, passing_of = [], [], []
    waits = {
        1: [near_in, far_in],
        2: [layer_out],
        4: [near_half],
        5: [far_half, near_hops[0]],
        6: [near_hops[1], far_hops[0]],
        7: [near_hops[2], far_hops[1]],
    }
    for b in range(batch):
        dq = None
        extra = out_t[b]
        passing = None
        for t in list(range(1, n_seq)) + [0]:
            first, last = t == 1, t == 0
            step = len(theirs_of)
            waiting = waits.get(step, [])
            waiting = waiting + theirs_of[max(step - 2, 0) : max(step - 1, 0)]
            waiting = waiting + across_of[max(step - 3, 0) : max(step - 2, 0)]
            lag = 2 if step == batch * n_seq - 1 else 3
            waiting = waiting + passing_of[max(step - lag, 0) : max(step - lag + 1, 0)]
            held = after(info, *waiting) if waiting else info
            outs = list(
                attend_back(
                    first, last, b, t, batch, held, segs, hidden_blocks[t][b], back[b], weight_kv,
                    queries[b], key_values[t][b], lse[b], extra, dq, sums, weight_q, more,
                )
            )
            keep, send = outs[:2]
            if step and step <= len(hops):
                axis, bit = hops[step - 1]
                small = small + flip(after(small, keep), axis, bit)
            sums = outs[2:4]
            if first:
                extra = outs[4]
            if last:
                more = outs[4:6]
            else:
                dq = outs[-1]
            theirs = flip(send, "mp", 1)
            theirs_of.append(theirs)
            across = flip(low_sum(keep[share:], theirs[share:]), "mp", 2)
            across_of.append(across)
            rows = keep[:share].astype(F32) + theirs[:share].astype(F32) + across.astype(F32)
            if passing is not None:
                rows = rows + onward(passing).astype(F32)
            passing = rows.astype(LOW)
            passing_of.append(passing)
        piece = (grad_first[b * share : (b + 1) * share] + rows).astype(LOW)
        input_grad = assemble(info, share_over_mp(piece), batch, share, F32, b, input_grad)
    for axis, bit in hops[batch * n_seq - 1 :]:
        small = small + flip(small, axis, bit)
    norm_small, up_bias_grad = small[:8], small[8]
    gq, q_sum = more
    gkv, v_sum = sums
    finished = finish_qkv(halves, info, gq, gkv)
    if halves:
        grad_qkv = low_sum(finished[0], flip(after(finished[1], theirs_of[-1]), "dp", 1))
    else:
        grad_qkv = lax.psum_scatter(finished[0], "dp", scatter_dimension=0, tiled=True)
    qkv_owned = ring_sum(grad_qkv)[-1][:, : 3 * inner].reshape(shard_rows, 3, inner)
    qv_bias_grad = over_groups(after(jnp.concatenate([q_sum[:1], v_sum[:1]], 0), theirs_of[-1]))
    return (
        layer_out,
        input_grad,
        qkv_owned,
        qv_bias_grad,
        proj_owned,
        norm_small[3],
        norm_small[4],
        norm_small[5],
        up_owned,
        up_bias_grad,
        down_owned,
        norm_small[0],
        norm_small[1],
        norm_small[2],
    )


def solution(mesh):
    in_specs = (
        P("dp", "seq", None),
        P("dp", "seq"),
        P("dp", "seq", None),
        P(("dp", "seq"), None, "mp"),
        P(None, "mp"),
        P(("dp", "seq"), "mp"),
        P(),
        P(),
        P(),
        P(("dp", "seq"), "mp"),
        P("mp"),
        P(("dp", "seq"), "mp"),
        P(),
        P(),
        P(),
    )
    out_specs = (
        P("dp", "seq", None),
        P("dp", "seq", None),
        P(("dp", "seq"), None, "mp"),
        P(None, "mp"),
        P(("dp", "seq"), "mp"),
        P(),
        P(),
        P(),
        P(("dp", "seq"), "mp"),
        P("mp"),
        P(("dp", "seq"), "mp"),
        P(),
        P(),
        P(),
    )
    return jax.shard_map(shards, mesh=mesh, in_specs=in_specs, out_specs=out_specs, check_vma=False)
```
